32 devices in a mesh: groups: 2 (over y), rollout: 8 (over z, x), tensor: 2 (over core).
Axes of the slice: x: 2, y: 2, z: 4, core: 2. Of those that a mesh axis runs over, the one named last changes fastest.
Arguments:
- hidden: bfloat16 [4, 3072, 8192], P(None, ('groups', 'rollout'), 'tensor'), parts along dimension 1, may hold values from -6 to 6
- counts: int32 [128], P('groups'), parts along dimension 0, may hold values from 1 to 72, 1536 in all
- key_value_weight: bfloat16 [8192, 2048], P('tensor'), may hold values from -0.09375 to 0.09375
- down_factor_weight: bfloat16 [128, 32, 8192], P(('groups', 'rollout'), None, 'tensor'), parts along dimension 0, may hold values from -0.0625 to 0.0625
- up_factor_weight: bfloat16 [128, 32, 2048], P(('groups', 'rollout'), None, 'tensor'), parts along dimension 0, may hold values from -1 to 1
Outputs:
- kv_new: bfloat16 [2048, 4, 3072], P('tensor', None, ('groups', 'rollout')), parts along dimension 2
The draws below stay inside these ranges and needn't reach their ends.
There are 2 independent parts, one for each index of `groups`. The reference program is written for one: setup_inputs(seed, part) draws one part's arguments, and reference() takes and returns one part's arrays. A program takes and returns all parts, laid end to end along the dimension named above; an argument that names none is the same for every part. Nothing has to cross between parts.
Inputs may be any that keep to these rules, and one draw needn't show every extreme that they name: counts sum to 1536; rows are stored grouped by adapter in increasing adapter order, adapter a holding the counts[a] rows after those of adapters 0 to a-1.
All inputs are finite; a program needn't handle non-finite values.
Results may differ from the reference program's by a relative error of at most 0.0095.
Values may be sent and summed in bfloat16 or wider, within the bound.
No kernel may reach another device: no remote copies, remote signals or barrier semaphores. Data moves between devices by JAX's collectives and lax.ppermute only.
A program may use at most 128 MiB of HBM per device.

```python
import math
import jax
import jax.numpy as jnp
import numpy as np
from jax import lax

MODEL_WIDTH = 8192
KEY_VALUE_COLS = 2048
ADAPTER_RANK = 32
ADAPTER_TOTAL = 64
DECODE_STEPS = 4
ROLLOUT_ROWS = 1536
MOST = 72
N_ROLLOUT = 8
N_TENSOR = 2


def strengthened(drawn, key, source, target, parts, factor):
    owner, partner = [(jnp.arange(drawn.shape[dim]) // (drawn.shape[dim] // parts)).reshape([-1 if axis == dim else 1 for axis in range(drawn.ndim)]) for dim in (source, target)]
    chosen = jax.random.permutation(key, parts)[partner]
    strong = (owner == chosen) | (owner == (partner + parts // 2) % parts)
    return jnp.where(strong, factor * drawn, drawn)


def block_scale(rng, extent, split, smallest, top_value):
    def one(position, shards_of):
        steps = jax.random.uniform(jax.random.fold_in(jax.random.fold_in(rng, 6), position), (shards_of,), jnp.float32, smallest / len(split), top_value / len(split))
        return jnp.repeat(jnp.exp(steps), extent[position] // shards_of).reshape((-1,) + (1,) * (len(extent) - position - 1))

    loudness = one(*split[0])
    for cut in split[1:]:
        loudness = loudness * one(*cut)
    return loudness


def profile(number_of, total, reach, lean):
    loads = [(1 << 20) // math.isqrt(standing ** lean) + 1 for standing in range(2, number_of + 1)]
    spare, holding = total - reach - (number_of - 1), [1] * (number_of - 1)
    while spare > 0:
        free = [i for i in range(number_of - 1) if holding[i] < reach]
        mass, remaining = sum([loads[i] for i in free]), spare
        for i in free:
            addition = min(reach - holding[i], max(1, remaining * loads[i] // mass), spare)
            holding[i] = holding[i] + addition
            spare = spare - addition
    return np.array([reach] + holding)


def ragged_sizes(key, count, total, bound, lean):
    if count == 2:
        one = jax.random.randint(key, (), max(1, total - bound), min(bound, total - 1) + 1)
        return jnp.stack([one, total - one])
    lengths = jnp.asarray(profile(count, total, bound, lean), jnp.int32)
    couples = (count - 1) // 2
    donor, taker = lengths[1:1 + 2 * couples:2], lengths[2:2 + 2 * couples:2]
    margin = jnp.minimum(donor - 1, bound - taker)
    shifted = jax.random.randint(jax.random.fold_in(key, 1), (couples,), 0, 1 << 20) % (margin + 1)
    lengths = lengths.at[1:1 + 2 * couples:2].set(donor - shifted).at[2:2 + 2 * couples:2].set(taker + shifted)
    return lengths[jax.random.permutation(jax.random.fold_in(key, 2), count)]


def scatter_about(rng, dims, width, most, split=(), held_as=jnp.bfloat16):
    loudness = block_scale(rng, dims, split, -0.22, 0.18) if split else 1.0
    result = jax.random.normal(rng, dims, jnp.float32) * width * loudness
    return jnp.minimum(jnp.maximum(result, -most), most).astype(held_as)


def heavy_noise(own_key, extent, width, most, cuts, heavy, kind=jnp.bfloat16):
    drawn = width * jax.random.normal(own_key, extent, jnp.float32)
    if cuts:
        drawn = drawn * block_scale(own_key, extent, cuts, -0.22, 0.18)
    return jnp.clip(strengthened(drawn, jax.random.fold_in(own_key, 3), *heavy), -most, most).astype(kind)


def setup_inputs(seed: int = 0, part: int = 0) -> dict:
    key_of = jax.random.split(jax.random.key(seed), 6)
    own_keys = jax.random.split(jax.random.fold_in(key_of[5], part), 6)
    return {
        "hidden": scatter_about(own_keys[0], (DECODE_STEPS, ROLLOUT_ROWS, MODEL_WIDTH), 1.0, 6.0, ((1, 8), (2, 2))),
        "counts": ragged_sizes(own_keys[1], ADAPTER_TOTAL, ROLLOUT_ROWS, MOST, 2).astype(jnp.int32),
        "key_value_weight": heavy_noise(key_of[2], (MODEL_WIDTH, KEY_VALUE_COLS), MODEL_WIDTH ** -0.5, 0.09375, ((0, 2),), (0, 1, 2, 2.0)),
        "down_factor_weight": scatter_about(own_keys[3], (ADAPTER_TOTAL, ADAPTER_RANK, MODEL_WIDTH), MODEL_WIDTH ** -0.5, 0.0625, ((0, 8), (2, 2))),
        "up_factor_weight": scatter_about(own_keys[4], (ADAPTER_TOTAL, ADAPTER_RANK, KEY_VALUE_COLS), ADAPTER_RANK ** -0.5, 1.0, ((0, 8), (2, 2))),
    }


def row_adapters(counts, row_total):
    bounds = jnp.cumsum(counts).astype(jnp.int32)
    positions = jnp.arange(row_total, dtype=jnp.int32)
    return jnp.sum((bounds[None, :] <= positions[:, None]).astype(jnp.int32), axis=1).astype(jnp.int32)


def reference(hidden, counts, key_value_weight, down_factor_weight, up_factor_weight):
    adapter = row_adapters(counts, ROLLOUT_ROWS)
    per_owner = ADAPTER_TOTAL // N_ROLLOUT
    slot_index = ((adapter % N_ROLLOUT) * per_owner + adapter // N_ROLLOUT).astype(jnp.int32)
    block_width = MODEL_WIDTH // N_TENSOR
    flat_rows = hidden.reshape(DECODE_STEPS * ROLLOUT_ROWS, MODEL_WIDTH)
    shared_output = jnp.zeros((DECODE_STEPS * ROLLOUT_ROWS, KEY_VALUE_COLS), jnp.float32)
    for block_index in range(N_TENSOR):
        partial_value = jnp.dot(flat_rows[:, block_index * block_width:(block_index + 1) * block_width],
                          key_value_weight[block_index * block_width:(block_index + 1) * block_width],
                          preferred_element_type=jnp.float32)
        rounded = lax.optimization_barrier(partial_value.astype(jnp.bfloat16))
        shared_output = shared_output + rounded.astype(jnp.float32)
    shared_output = shared_output.reshape(DECODE_STEPS, ROLLOUT_ROWS, KEY_VALUE_COLS)

    def one_block(pair):
        rows_block, slot_block = pair
        down_factor_rows = down_factor_weight[slot_block].astype(jnp.float32)
        rank_proj = jnp.einsum('srd,rkd->srk', rows_block.astype(jnp.float32), down_factor_rows,
                               precision=lax.Precision.HIGHEST)
        up_factor_rows = up_factor_weight[slot_block].astype(jnp.float32)
        return jnp.einsum('srk,rkc->src', rank_proj, up_factor_rows, precision=lax.Precision.HIGHEST)

    blocked = hidden.reshape(DECODE_STEPS, ROLLOUT_ROWS // 8, 8, MODEL_WIDTH).transpose(1, 0, 2, 3)
    slot_blocks = slot_index.reshape(ROLLOUT_ROWS // 8, 8)
    adapter_deltas = lax.map(one_block, (blocked, slot_blocks))
    low_rank_delta = adapter_deltas.transpose(1, 0, 2, 3).reshape(DECODE_STEPS, ROLLOUT_ROWS, KEY_VALUE_COLS)
    combined_output = shared_output + low_rank_delta
    return combined_output.astype(jnp.bfloat16).transpose(2, 0, 1)
```

```python
import jax
import jax.numpy as jnp
from jax import lax
from jax.sharding import PartitionSpec as P

PAIR_SLOTS = 3
FORWARD_SLOTS = 2
BF16 = jnp.bfloat16
F32 = jnp.float32
I32 = jnp.int32


def count_at_most(bounds, rows):
    return jnp.sum((bounds <= rows[..., None]).astype(I32), axis=-1)


def first_slot(owner, adapter, owners):
    return (adapter - owner + owners - 1) // owners


def end_slot(owner, adapter, owners):
    return (adapter - owner + owners) // owners


def slots_of(stored, start, size):
    return lax.dynamic_slice_in_dim(stored, start, size, axis=0)


def send(value, hop, owners):
    return lax.ppermute(value, "rollout", [(i, i ^ hop) for i in range(owners)])


def scores(hidden, factors, mask):
    every = jnp.einsum("srd,nkd->srnk", hidden, factors, preferred_element_type=F32)
    return jnp.sum(every * mask[None, :, :, None].astype(F32), axis=2)


def expand(rank_proj, mask):
    wide = rank_proj.astype(BF16)[:, :, None, :] * mask[None, :, :, None].astype(BF16)
    return wide.reshape(wide.shape[:2] + (-1,))


def delta(rank_proj, factors, mask):
    return jnp.einsum(
        "srw,wc->src",
        expand(rank_proj, mask),
        factors.reshape(-1, factors.shape[2]),
        preferred_element_type=F32,
    )


def local(hidden, counts, key_value_weight, down, up):
    steps, rows, width = hidden.shape
    adapters = counts.shape[0]
    owners = lax.axis_size("rollout")
    sides = lax.axis_size("tensor")
    held = down.shape[0]
    pair_slots = min(PAIR_SLOTS, held)
    forward_slots = min(FORWARD_SLOTS, pair_slots)
    me = lax.axis_index("rollout")
    side = lax.axis_index("tensor")

    order = jnp.arange(adapters, dtype=I32)
    bounds = jnp.sum(jnp.where(order[:, None] <= order[None, :], counts[:, None], 0), axis=0)
    row_adapter = count_at_most(bounds, me * rows + jnp.arange(rows, dtype=I32))
    device = jnp.arange(owners, dtype=I32)
    low = count_at_most(bounds, device * rows)
    high = count_at_most(bounds, device * rows + (rows - 1))
    owner = device[:, None]
    low_pair = low[device // 2 * 2]
    pair_start = jnp.minimum(first_slot(owner, low_pair[None, :], owners), held - pair_slots)
    forward_start = jnp.minimum(
        first_slot(owner, low[None, :], owners), pair_start + (pair_slots - forward_slots)
    )
    same_column = (owner % 2) == (device[None, :] % 2)
    covered = jnp.where(same_column, pair_start + pair_slots, forward_start + forward_slots)
    extra = jnp.max(jnp.maximum(end_slot(owner, high[None, :], owners) - covered, 0))
    group_count = lax.axis_size("groups")
    rounds = extra
    for turn in range(1, group_count):
        rounds = jnp.maximum(
            rounds,
            lax.ppermute(
                extra, "groups", [(i, (i + turn) % group_count) for i in range(group_count)]
            ),
        )

    hops = [2 * m for m in range(owners // 2)]

    def exchanged(stored):
        kept = []
        for hop in hops:
            if hop == 0:
                kept.append(slots_of(stored, pair_start[me, me], pair_slots))
            else:
                kept.append(
                    send(slots_of(stored, pair_start[me, me ^ hop], pair_slots), hop, owners)
                )
        passed = []
        for hop, block in zip(hops, kept):
            source = me ^ hop
            offset = forward_start[source, me ^ 1] - pair_start[source, me]
            passed.append(send(slots_of(block, offset, forward_slots), 1, owners))
        return kept, passed

    def slot_mask(source, start, size):
        ids = source + owners * (start + jnp.arange(size, dtype=I32))
        return row_adapter[:, None] == ids[None, :]

    kept_masks = [slot_mask(me ^ hop, pair_start[me ^ hop, me], pair_slots) for hop in hops]
    passed_masks = [
        slot_mask(me ^ 1 ^ hop, forward_start[me ^ 1 ^ hop, me], forward_slots) for hop in hops
    ]
    masks = kept_masks + passed_masks

    kept, passed = exchanged(down)
    kept_up, passed_up = exchanged(up)

    own_columns = key_value_weight.shape[1] // sides
    if sides == 2:
        theirs = lax.dynamic_slice_in_dim(
            key_value_weight, (1 - side) * own_columns, own_columns, axis=1
        )
        mine = lax.dynamic_slice_in_dim(key_value_weight, side * own_columns, own_columns, axis=1)
        base_sent = jnp.einsum(
            "srd,dc->src", hidden, theirs, preferred_element_type=F32
        ).astype(BF16)
        base_got = lax.ppermute(base_sent, "tensor", [(0, 1), (1, 0)])
        base_mine = jnp.einsum("srd,dc->src", hidden, mine, preferred_element_type=F32).astype(BF16)

        def base():
            return base_mine.astype(F32) + base_got.astype(F32)
    else:
        base_all = jnp.einsum(
            "srd,dc->src", hidden, key_value_weight, preferred_element_type=F32
        ).astype(BF16)
        base_sum = lax.psum_scatter(base_all, "tensor", scatter_dimension=2, tiled=True)

        def base():
            return base_sum.astype(F32)

    rank_part = None
    for block, mask in zip(kept + passed, masks):
        part = scores(hidden, block, mask)
        rank_part = part if rank_part is None else rank_part + part

    def round_blocks(stored, turn):
        blocks, valid = [], []
        for hop in range(owners):
            wanted = covered[me, me ^ hop] + turn
            block = slots_of(stored, jnp.minimum(wanted, held - 1), 1)
            blocks.append(block if hop == 0 else send(block, hop, owners))
            source = me ^ hop
            slot = covered[source, me] + turn
            valid.append(jnp.where(slot < held, source + owners * slot, -1))
        return jnp.concatenate(blocks), row_adapter[:, None] == jnp.stack(valid)[None, :]

    def more_rank(turn, total):
        blocks, mask = round_blocks(down, turn)
        return total + scores(hidden, blocks, mask)

    rank_part = lax.fori_loop(0, rounds, more_rank, rank_part)

    if sides == 2:
        rank_proj = rank_part + lax.ppermute(
            rank_part.astype(BF16), "tensor", [(0, 1), (1, 0)]
        ).astype(F32)
    else:
        rank_proj = lax.psum(rank_part.astype(BF16), "tensor").astype(F32)

    all_up = jnp.concatenate(kept_up + passed_up)
    all_mask = jnp.concatenate(masks, axis=1)

    def first():
        return base() + delta(rank_proj, all_up, all_mask)

    def finish(total):
        return total.astype(BF16)

    def more_delta(turn, total):
        blocks, mask = round_blocks(up, turn)
        return total + delta(rank_proj, blocks, mask)

    out = lax.cond(
        rounds > 0,
        lambda: finish(lax.fori_loop(0, rounds, more_delta, first())),
        lambda: finish(first()),
    )
    return out.transpose(2, 0, 1)


def solution(mesh):
    placed = (
        P(None, ("groups", "rollout"), "tensor"),
        P("groups"),
        P("tensor", None),
        P(("groups", "rollout"), None, "tensor"),
        P(("groups", "rollout"), None, "tensor"),
    )
    return jax.shard_map(
        local,
        mesh=mesh,
        in_specs=placed,
        out_specs=P("tensor", None, ("groups", "rollout")),
        check_vma=False,
    )
```

```python
import functools

import jax
import jax.numpy as jnp
from jax import lax
from jax.experimental import pallas as pl
from jax.experimental.pallas import tpu as pltpu
from jax.sharding import PartitionSpec as P

PAIR_SLOTS = 3
FORWARD_SLOTS = 2
LANES = 128
VMEM_LIMIT = 48 * 1024 * 1024
BF16 = jnp.bfloat16
F32 = jnp.float32
I32 = jnp.int32
SMALL = pl.CostEstimate(flops=1000, bytes_accessed=1000, transcendentals=0)
PARAMS = pltpu.CompilerParams(vmem_limit_bytes=VMEM_LIMIT)
IN_SMEM = pl.BlockSpec(memory_space=pltpu.SMEM)
ANYWHERE = pl.BlockSpec(memory_space=pl.ANY)


def first_slot(owner, adapter, owners):
    return lax.div(adapter - owner + (owners - 1), jnp.int32(owners))


def end_slot(owner, adapter, owners):
    return lax.div(adapter - owner + owners, jnp.int32(owners))


def pair_start(owner, low_pair, sizes):
    return jnp.minimum(first_slot(owner, low_pair, sizes.owners), sizes.held - sizes.kept)


def forward_start(owner, low, low_pair, sizes):
    return jnp.minimum(
        first_slot(owner, low, sizes.owners),
        pair_start(owner, low_pair, sizes) + (sizes.kept - sizes.passed),
    )


class Sizes:
    def __init__(self, owners, adapters, held, rows):
        self.owners, self.adapters, self.held, self.rows = owners, adapters, held, rows
        self.kept = min(PAIR_SLOTS, held)
        self.passed = min(FORWARD_SLOTS, self.kept)
        self.pairs = owners // 2
        self.slots = self.pairs * (self.kept + self.passed)

    def kept_base(self, m):
        return m * self.kept

    def passed_base(self, m):
        return self.pairs * self.kept + m * self.passed


def pack_kernel(sizes, counts, stored, *refs):
    pairs = sizes.pairs
    sent, (passed0, bounds, windows, low_pair, sems) = refs[: pairs - 1], refs[pairs - 1 :]
    me = lax.axis_index("rollout")
    mine = lax.div(me, jnp.int32(2))
    odd_row = (2 * mine + 1) * sizes.rows
    bounds[0] = jnp.int32(0)

    def add(a, carry):
        end = carry[0] + counts[a]
        bounds[a + 1] = end
        lows = [
            low + (end <= 2 * p * sizes.rows).astype(I32) for p, low in enumerate(carry[1 : pairs + 1])
        ]
        return (end, *lows, carry[pairs + 1] + (end <= odd_row).astype(I32))

    found = lax.fori_loop(0, sizes.adapters, add, (jnp.int32(0),) * (pairs + 2), unroll=8)
    for p in range(pairs):
        low_pair[p] = found[1 + p]
    odd = found[pairs + 1]
    low_mine = low_pair[mine]
    is_even = me == 2 * mine
    low_other = jnp.where(is_even, odd, low_mine)
    copies = []
    for m in range(1, pairs):
        start = pair_start(me, low_pair[mine ^ m], sizes)
        windows[m] = start
        copies.append(
            pltpu.make_async_copy(stored.at[pl.ds(start, sizes.kept)], sent[m - 1], sems.at[m])
        )
    start = forward_start(me, low_other, low_mine, sizes)
    copies.insert(
        0, pltpu.make_async_copy(stored.at[pl.ds(start, sizes.passed)], passed0, sems.at[0])
    )
    for copy in copies:
        copy.start()
    windows[pairs] = start
    windows[0] = pair_start(me, low_mine, sizes)
    for m in range(pairs):
        source = me ^ (2 * m)
        windows[pairs + 1 + m] = forward_start(source, low_other, low_mine, sizes) - pair_start(
            source, low_mine, sizes
        )
    windows[2 * pairs + 1] = low_mine
    windows[2 * pairs + 2] = jnp.where(is_even, low_mine, odd)
    for copy in copies:
        copy.wait()


def pack(sizes, counts, stored):
    tail = stored.shape[1:]
    block = jax.ShapeDtypeStruct((sizes.kept,) + tail, stored.dtype)
    small = jax.ShapeDtypeStruct((sizes.passed,) + tail, stored.dtype)
    pairs = sizes.pairs
    return pl.pallas_call(
        functools.partial(pack_kernel, sizes),
        out_shape=[block] * (pairs - 1)
        + [
            small,
            jax.ShapeDtypeStruct((sizes.adapters + 1,), I32),
            jax.ShapeDtypeStruct((2 * pairs + 3,), I32),
        ],
        in_specs=[IN_SMEM, ANYWHERE],
        out_specs=[ANYWHERE] * pairs + [IN_SMEM, IN_SMEM],
        scratch_shapes=[pltpu.SMEM((pairs,), I32), pltpu.SemaphoreType.DMA((pairs,))],
        compiler_params=PARAMS,
        cost_estimate=SMALL,
        name="pack",
    )(counts, stored)


def pack_again_kernel(sizes, windows, stored, *refs):
    pairs = sizes.pairs
    sent, (passed0, kept0, sems) = refs[: pairs - 1], refs[pairs - 1 :]
    copies = [
        pltpu.make_async_copy(stored.at[pl.ds(windows[m], sizes.kept)], target, sems.at[m])
        for m, target in enumerate((kept0,) + tuple(sent))
    ]
    copies.append(
        pltpu.make_async_copy(
            stored.at[pl.ds(windows[pairs], sizes.passed)], passed0, sems.at[pairs]
        )
    )
    for copy in copies:
        copy.start()
    for copy in copies:
        copy.wait()


def pack_again(sizes, windows, stored):
    tail = stored.shape[1:]
    block = jax.ShapeDtypeStruct((sizes.kept,) + tail, stored.dtype)
    small = jax.ShapeDtypeStruct((sizes.passed,) + tail, stored.dtype)
    pairs = sizes.pairs
    return pl.pallas_call(
        functools.partial(pack_again_kernel, sizes),
        out_shape=[block] * (pairs - 1) + [small, block],
        in_specs=[IN_SMEM, ANYWHERE],
        out_specs=[ANYWHERE] * (pairs + 1),
        scratch_shapes=[pltpu.SemaphoreType.DMA((pairs + 1,))],
        compiler_params=PARAMS,
        cost_estimate=SMALL,
        name="pack_again",
    )(windows, stored)


def cut_kernel(index, size, windows, block, out, sem):
    copy = pltpu.make_async_copy(block.at[pl.ds(windows[index], size)], out, sem)
    copy.start()
    copy.wait()


def cut(windows, index, block, size):
    return pl.pallas_call(
        functools.partial(cut_kernel, index, size),
        out_shape=jax.ShapeDtypeStruct((size,) + block.shape[1:], block.dtype),
        in_specs=[IN_SMEM, ANYWHERE],
        out_specs=ANYWHERE,
        scratch_shapes=[pltpu.SemaphoreType.DMA],
        compiler_params=PARAMS,
        cost_estimate=SMALL,
        name="cut",
    )(windows, block)


def ranges_kernel(sizes, bounds, windows, ranges, rounds, lows, highs):
    me = lax.axis_index("rollout")
    low_mine = windows[2 * sizes.pairs + 1]
    low = windows[2 * sizes.pairs + 2]
    first_row = me * sizes.rows

    def fill(base, source, start, size):
        for k in range(size):
            adapter = source + sizes.owners * (start + k)
            ranges[2 * (base + k)] = bounds[adapter] - first_row
            ranges[2 * (base + k) + 1] = bounds[adapter + 1] - first_row

    for m in range(sizes.pairs):
        source = me ^ (2 * m)
        fill(sizes.kept_base(m), source, pair_start(source, low_mine, sizes), sizes.kept)
        source = me ^ 1 ^ (2 * m)
        fill(sizes.passed_base(m), source, forward_start(source, low, low_mine, sizes), sizes.passed)

    for d in range(sizes.owners):
        lows[d] = jnp.int32(0)
        highs[d] = jnp.int32(0)

    def count(a, carry):
        end = bounds[a + 1]
        return tuple(
            c + (end <= d * sizes.rows + last).astype(I32)
            for (d, last), c in zip(places, carry)
        )

    places = [(d, last) for last in (0, sizes.rows - 1) for d in range(sizes.owners)]
    found = lax.fori_loop(0, sizes.adapters, count, (jnp.int32(0),) * len(places))
    for d in range(sizes.owners):
        lows[d] = found[d]
        highs[d] = found[sizes.owners + d]

    def most(d, so_far):
        low_d, high_d, low_p = lows[d], highs[d], lows[lax.div(d, jnp.int32(2)) * 2]

        def each(owner, so_far):
            same = ((owner ^ d) & 1) == 0
            covered = jnp.where(
                same,
                pair_start(owner, low_p, sizes) + sizes.kept,
                forward_start(owner, low_d, low_p, sizes) + sizes.passed,
            )
            return jnp.maximum(so_far, end_slot(owner, high_d, sizes.owners) - covered)

        return lax.fori_loop(0, sizes.owners, each, so_far)

    rounds[0] = lax.fori_loop(0, sizes.owners, most, jnp.int32(0))


def ranges_of(sizes, bounds, windows):
    return pl.pallas_call(
        functools.partial(ranges_kernel, sizes),
        out_shape=[
            jax.ShapeDtypeStruct((2 * sizes.slots,), I32),
            jax.ShapeDtypeStruct((1,), I32),
        ],
        in_specs=[IN_SMEM, IN_SMEM],
        out_specs=[IN_SMEM, IN_SMEM],
        scratch_shapes=[pltpu.SMEM((sizes.owners,), I32), pltpu.SMEM((sizes.owners,), I32)],
        compiler_params=PARAMS,
        cost_estimate=SMALL,
        name="ranges",
    )(bounds, windows)


def lane_mask(ranges, base, size, rank, rows, steps):
    lane = lax.broadcasted_iota(I32, (1, size * rank), 1)
    low = jnp.zeros((1, size * rank), I32)
    high = jnp.zeros((1, size * rank), I32)
    for k in range(size):
        here = (lane >= k * rank) & (lane < (k + 1) * rank)
        low = jnp.where(here, ranges[2 * (base + k)], low)
        high = jnp.where(here, ranges[2 * (base + k) + 1], high)
    row = lax.broadcasted_iota(I32, (rows, size * rank), 0)
    one = (row >= low) & (row < high)
    return jnp.concatenate([one] * steps, axis=0) if steps > 1 else one


def scores_kernel(bases, rank, rows, fold, with_before, ranges, hidden, *refs):
    blocks, refs = refs[: len(bases)], refs[len(bases) :]
    before, refs = (refs[0], refs[1:]) if with_before else (None, refs)
    out = refs[0]
    sent = refs[1] if fold else None
    sums = refs[-len(bases) :]
    k = pl.program_id(0)
    steps = hidden.shape[0] // rows

    for block, total in zip(blocks, sums):
        part = lax.dot_general(
            hidden[...], block[...], (((1,), (1,)), ((), ())), preferred_element_type=F32
        )

        @pl.when(k == 0)
        def _(total=total, part=part):
            total[...] = part

        @pl.when(k > 0)
        def _(total=total, part=part):
            total[...] += part

    @pl.when(k == pl.num_programs(0) - 1)
    def _():
        for s in range(steps):
            here = pl.ds(s * rows, rows)
            acc = before[here, :] if with_before else jnp.zeros((rows, LANES), F32)
            for base, total in zip(bases, sums):
                wide = total.shape[1]
                masked = jnp.where(
                    lane_mask(ranges, base, wide // rank, rank, rows, 1), total[here, :], 0.0
                )
                if wide < LANES:
                    masked = jnp.concatenate(
                        [masked, jnp.zeros((rows, LANES - wide), F32)], axis=1
                    )
                acc = acc + masked
            if fold:
                shift = LANES // 2
                while shift >= rank:
                    acc = acc + pltpu.roll(acc, shift, 1)
                    shift //= 2
                sent[here, :] = acc.astype(BF16)
            out[here, :] = acc


def scores(ranges, hidden, blocks, bases, rows, before=None, fold=False):
    total_rows, width = hidden.shape
    rank = blocks[0].shape[1]
    tiles = 4 if width % 512 == 0 and width >= 2048 else 1
    tile = width // tiles
    flat = [b.reshape(-1, width) for b in blocks]
    whole = pl.BlockSpec((total_rows, LANES), lambda k: (0, 0))
    out_shape = [jax.ShapeDtypeStruct((total_rows, LANES), F32)]
    if fold:
        out_shape.append(jax.ShapeDtypeStruct((total_rows, LANES), BF16))
    with_before = before is not None
    return pl.pallas_call(
        functools.partial(scores_kernel, bases, rank, rows, fold, with_before),
        grid=(tiles,),
        out_shape=out_shape,
        in_specs=[IN_SMEM, pl.BlockSpec((total_rows, tile), lambda k: (0, k))]
        + [pl.BlockSpec((f.shape[0], tile), lambda k: (0, k)) for f in flat]
        + [whole] * with_before,
        out_specs=[whole] * len(out_shape),
        scratch_shapes=[pltpu.VMEM((total_rows, f.shape[0]), F32) for f in flat],
        compiler_params=PARAMS,
        cost_estimate=SMALL,
        name="scores",
    )(ranges, hidden, *flat, *([before] if with_before else []))


def base_kernel(which, hidden, weight, out):
    out[...] = jnp.dot(hidden[...], weight[...], preferred_element_type=F32).astype(BF16)


def base_product(which, hidden, weight, columns):
    total_rows, width = hidden.shape
    tile = min(256, columns)
    tiles = columns // tile
    return pl.pallas_call(
        base_kernel,
        grid_spec=pltpu.PrefetchScalarGridSpec(
            num_scalar_prefetch=1,
            grid=(tiles,),
            in_specs=[
                pl.BlockSpec((total_rows, width), lambda j, which: (0, 0)),
                pl.BlockSpec((width, tile), lambda j, which: (0, which[0] * tiles + j)),
            ],
            out_specs=pl.BlockSpec((total_rows, tile), lambda j, which: (0, j)),
        ),
        out_shape=jax.ShapeDtypeStruct((total_rows, columns), BF16),
        compiler_params=PARAMS,
        cost_estimate=SMALL,
        name="base_product",
    )(which, hidden, weight)


def final_kernel(bases, rank, rows, n_added, ranges, own, *refs):
    got, refs = refs[0], refs[1:]
    added, refs = refs[:n_added], refs[n_added:]
    blocks, (out, left, right) = refs[: len(bases)], refs[len(bases) :]
    group = LANES // rank
    slots = sum(b.shape[0] for b in blocks) // rank
    steps = own.shape[0] // rows

    @pl.when(pl.program_id(0) == 0)
    def _():
        for s in range(steps):
            here = pl.ds(s * rows, rows)
            proj = (own[here, :] + got[here, :].astype(F32)).astype(BF16)
            for g in range(left.shape[1] // LANES):
                size = min(group, slots - g * group)
                mask = lane_mask(ranges, g * group, size, rank, rows, 1)
                part = jnp.where(mask, proj[:, : size * rank].astype(F32), 0.0)
                if size < group:
                    part = jnp.concatenate(
                        [part, jnp.zeros((rows, LANES - size * rank), F32)], axis=1
                    )
                left[here, g * LANES : (g + 1) * LANES] = part.astype(BF16)
        right[...] = jnp.zeros_like(right)

    for base, block in zip(bases, blocks):
        right[base * rank : base * rank + block.shape[0], :] = block[...]
    total = jnp.dot(left[...], right[...], preferred_element_type=F32)
    for term in added:
        total = total + term[...].astype(F32)
    out[...] = total.astype(BF16)


def final(ranges, own, got, added, blocks, bases, rows):
    total_rows = own.shape[0]
    rank, columns = blocks[0].shape[1:]
    flat = [b.reshape(-1, columns) for b in blocks]
    tile = min(256, columns)
    deep = -(-sum(f.shape[0] for f in flat) // LANES) * LANES
    whole = pl.BlockSpec((total_rows, LANES), lambda j: (0, 0))
    part = pl.BlockSpec((total_rows, tile), lambda j: (0, j))
    return pl.pallas_call(
        functools.partial(final_kernel, bases, rank, rows, len(added)),
        grid=(columns // tile,),
        out_shape=jax.ShapeDtypeStruct((total_rows, columns), BF16),
        in_specs=[IN_SMEM, whole, whole]
        + [part] * len(added)
        + [pl.BlockSpec((f.shape[0], tile), lambda j: (0, j)) for f in flat],
        out_specs=part,
        scratch_shapes=[pltpu.VMEM((total_rows, deep), BF16), pltpu.VMEM((deep, tile), BF16)],
        compiler_params=PARAMS,
        cost_estimate=SMALL,
        name="final",
    )(ranges, own, got, *added, *flat)


def send(value, hop, owners):
    return lax.ppermute(value, "rollout", [(i, i ^ hop) for i in range(owners)])


class Extra:

    def __init__(self, sizes, counts):
        rows, owners = sizes.rows, sizes.owners
        self.sizes = sizes
        self.me = lax.axis_index("rollout")
        order = jnp.arange(sizes.adapters, dtype=I32)
        bounds = jnp.sum(jnp.where(order[:, None] <= order[None, :], counts[:, None], 0), axis=0)

        def at_most(positions):
            return jnp.sum((bounds <= positions[:, None]).astype(I32), axis=-1)

        self.row_adapter = at_most(self.me * rows + jnp.arange(rows, dtype=I32))
        device = jnp.arange(owners, dtype=I32)
        low = at_most(device * rows)
        owner = device[:, None]
        low_pair = low[device // 2 * 2][None, :]
        self.covered = jnp.where(
            (owner % 2) == (device[None, :] % 2),
            pair_start(owner, low_pair, sizes) + sizes.kept,
            forward_start(owner, low[None, :], low_pair, sizes) + sizes.passed,
        )

    def blocks(self, stored, turn):
        sizes, me = self.sizes, self.me
        blocks, adapters = [], []
        for hop in range(sizes.owners):
            wanted = jnp.minimum(self.covered[me, me ^ hop] + turn, sizes.held - 1)
            block = lax.dynamic_slice_in_dim(stored, wanted, 1, axis=0)
            blocks.append(block if hop == 0 else send(block, hop, sizes.owners))
            source = me ^ hop
            slot = self.covered[source, me] + turn
            adapters.append(jnp.where(slot < sizes.held, source + sizes.owners * slot, -1))
        return jnp.concatenate(blocks), self.row_adapter[:, None] == jnp.stack(adapters)[None, :]

    def more_rank(self, hidden, down, turn, total):
        blocks, mask = self.blocks(down, turn)
        rank = blocks.shape[1]
        every = jnp.einsum("srd,nkd->srnk", hidden, blocks, preferred_element_type=F32)
        more = jnp.sum(every * mask[None, :, :, None].astype(F32), axis=2)
        return total + jnp.concatenate([more] * (LANES // rank), axis=2).reshape(total.shape)

    def more_delta(self, rank_proj, up, turn, total):
        blocks, mask = self.blocks(up, turn)
        wide = rank_proj[:, :, None, :] * mask[None, :, :, None].astype(BF16)
        wide = wide.reshape(wide.shape[:2] + (-1,))
        more = jnp.einsum(
            "srw,wc->src",
            wide,
            blocks.reshape(-1, blocks.shape[2]),
            preferred_element_type=F32,
        )
        return total + more.reshape(total.shape)


def local(hidden, counts, key_value_weight, down, up):
    steps, rows, width = hidden.shape
    owners = lax.axis_size("rollout")
    sides = lax.axis_size("tensor")
    held, rank = down.shape[:2]
    sizes = Sizes(owners, counts.shape[0], held, rows)
    pairs = sizes.pairs
    side = lax.axis_index("tensor")
    flat = hidden.reshape(steps * rows, width)
    own_columns = key_value_weight.shape[1] // sides

    *to_pairs, to_side, bounds, windows = pack(sizes, counts, down)
    from_pairs = [send(b, 2 * m, owners) for m, b in zip(range(1, pairs), to_pairs)]
    from_side = send(to_side, 1, owners)

    ranges, extra = ranges_of(sizes, bounds, windows)
    *to_pairs_up, to_side_up, kept_up = pack_again(sizes, windows, up)

    if sides == 2:
        side_index = jnp.reshape(side, (1,)).astype(I32)
        theirs = base_product(1 - side_index, flat, key_value_weight, own_columns)
        added = [
            lax.ppermute(theirs, "tensor", [(0, 1), (1, 0)]),
            base_product(side_index, flat, key_value_weight, own_columns),
        ]
    else:
        partial = jnp.dot(flat, key_value_weight, preferred_element_type=F32).astype(BF16)
        added = [lax.psum_scatter(partial, "tensor", scatter_dimension=1, tiled=True)]

    group_count = lax.axis_size("groups")
    rounds = extra
    for turn in range(1, group_count):
        around = [(i, (i + turn) % group_count) for i in range(group_count)]
        rounds = jnp.maximum(rounds, lax.ppermute(extra, "groups", around))
    more = rounds[0] > 0

    kept = [cut(windows, 0, down, sizes.kept)] + from_pairs
    passed = [from_side] + [
        send(cut(windows, pairs + 1 + m, block, sizes.passed), 1, owners)
        for m, block in zip(range(1, pairs), from_pairs)
    ]
    kept_bases = [sizes.kept_base(m) for m in range(pairs)]
    passed_bases = [sizes.passed_base(m) for m in range(pairs)]

    acc = None
    for m in range(pairs - 1):
        acc = scores(ranges, flat, [kept[m]], [kept_bases[m]], rows, acc)[0]
        acc = scores(ranges, flat, [passed[m]], [passed_bases[m]], rows, acc)[0]
    acc = scores(ranges, flat, [kept[-1]], [kept_bases[-1]], rows, acc)[0]
    own, sent = scores(ranges, flat, [passed[-1]], [passed_bases[-1]], rows, acc, fold=True)

    def all_rank():
        rest = Extra(sizes, counts)
        total = lax.fori_loop(
            0, rounds[0], functools.partial(rest.more_rank, hidden, down), own
        )
        return total, total.astype(BF16)

    own, sent = lax.cond(more, all_rank, lambda: (own, sent))
    if sides == 2:
        got = lax.ppermute(sent, "tensor", [(0, 1), (1, 0)])
    else:
        got = lax.psum(sent, "tensor")
        own = jnp.zeros_like(own)

    from_pairs_up = [send(b, 2 * m, owners) for m, b in zip(range(1, pairs), to_pairs_up)]
    kept_ups = [kept_up] + from_pairs_up
    passed_ups = [send(to_side_up, 1, owners)] + [
        send(cut(windows, pairs + 1 + m, block, sizes.passed), 1, owners)
        for m, block in zip(range(1, pairs), from_pairs_up)
    ]

    def finish(terms):
        return final(
            ranges, own, got, terms, kept_ups + passed_ups, kept_bases + passed_bases, rows
        )

    def all_delta():
        rest = Extra(sizes, counts)
        proj = (own + got.astype(F32)).astype(BF16)[:, :rank].reshape(steps, rows, rank)
        delta = lax.fori_loop(
            0,
            rounds[0],
            functools.partial(rest.more_delta, proj, up),
            jnp.zeros(added[0].shape, F32),
        )
        return finish(added + [delta])

    out = lax.cond(more, all_delta, lambda: finish(added))
    return out.reshape(steps, rows, own_columns).transpose(2, 0, 1)


def solution(mesh):
    placed = (
        P(None, ("groups", "rollout"), "tensor"),
        P("groups"),
        P("tensor", None),
        P(("groups", "rollout"), None, "tensor"),
        P(("groups", "rollout"), None, "tensor"),
    )
    return jax.shard_map(
        local,
        mesh=mesh,
        in_specs=placed,
        out_specs=P("tensor", None, ("groups", "rollout")),
        check_vma=False,
    )
```

```python
import functools

import jax
import jax.numpy as jnp
from jax import lax
from jax.experimental import pallas as pl
from jax.experimental.pallas import tpu as pltpu
from jax.sharding import PartitionSpec as P

PAIR_SLOTS = 3
FORWARD_SLOTS = 2
VMEM_LIMIT = 24 * 1024 * 1024
BF16 = jnp.bfloat16
F32 = jnp.float32
I32 = jnp.int32
SMALL = pl.CostEstimate(flops=1000, bytes_accessed=1000, transcendentals=0)
PARAMS = pltpu.CompilerParams(vmem_limit_bytes=VMEM_LIMIT)
IN_SMEM = pl.BlockSpec(memory_space=pltpu.SMEM)
IN_VMEM = pl.BlockSpec(memory_space=pltpu.VMEM)
ANYWHERE = pl.BlockSpec(memory_space=pl.ANY)


def first_slot(owner, adapter, owners):
    return lax.div(adapter - owner + (owners - 1), jnp.int32(owners))


def end_slot(owner, adapter, owners):
    return lax.div(adapter - owner + owners, jnp.int32(owners))


def pair_start(owner, low_pair, sizes):
    return jnp.minimum(first_slot(owner, low_pair, sizes.owners), sizes.held - sizes.kept)


def forward_start(owner, low, low_pair, sizes):
    return jnp.minimum(
        first_slot(owner, low, sizes.owners),
        pair_start(owner, low_pair, sizes) + (sizes.kept - sizes.passed),
    )


class Sizes:
    def __init__(self, owners, adapters, held, rows):
        self.owners, self.adapters, self.held, self.rows = owners, adapters, held, rows
        self.kept = min(PAIR_SLOTS, held)
        self.passed = min(FORWARD_SLOTS, self.kept)
        self.pairs = owners // 2
        self.slots = self.pairs * (self.kept + self.passed)

    def kept_base(self, m):
        return m * self.kept

    def passed_base(self, m):
        return self.pairs * self.kept + m * self.passed


def pack_kernel(sizes, counts, stored, *refs):
    pairs = sizes.pairs
    sent, (passed0, bounds, windows, low_pair, sems) = refs[: pairs - 1], refs[pairs - 1 :]
    me = lax.axis_index("rollout")
    mine = lax.div(me, jnp.int32(2))
    odd_row = (2 * mine + 1) * sizes.rows
    bounds[0] = jnp.int32(0)

    def add(a, carry):
        end = carry[0] + counts[a]
        bounds[a + 1] = end
        lows = [
            low + (end <= 2 * p * sizes.rows).astype(I32) for p, low in enumerate(carry[1 : pairs + 1])
        ]
        return (end, *lows, carry[pairs + 1] + (end <= odd_row).astype(I32))

    found = lax.fori_loop(0, sizes.adapters, add, (jnp.int32(0),) * (pairs + 2), unroll=8)
    for p in range(pairs):
        low_pair[p] = found[1 + p]
    odd = found[pairs + 1]
    low_mine = low_pair[mine]
    is_even = me == 2 * mine
    low_other = jnp.where(is_even, odd, low_mine)
    copies = []
    for m in range(1, pairs):
        start = pair_start(me, low_pair[mine ^ m], sizes)
        windows[m] = start
        copies.append(
            pltpu.make_async_copy(stored.at[pl.ds(start, sizes.kept)], sent[m - 1], sems.at[m])
        )
    start = forward_start(me, low_other, low_mine, sizes)
    copies.insert(
        0, pltpu.make_async_copy(stored.at[pl.ds(start, sizes.passed)], passed0, sems.at[0])
    )
    for copy in copies:
        copy.start()
    windows[pairs] = start
    windows[0] = pair_start(me, low_mine, sizes)
    for m in range(pairs):
        source = me ^ (2 * m)
        windows[pairs + 1 + m] = forward_start(source, low_other, low_mine, sizes) - pair_start(
            source, low_mine, sizes
        )
    windows[2 * pairs + 1] = low_mine
    windows[2 * pairs + 2] = jnp.where(is_even, low_mine, odd)
    for copy in copies:
        copy.wait()


def in_vmem(size, like):
    return pltpu.VMEM((size,) + like.shape[1:], like.dtype)


def held_in_vmem(value):
    return pltpu.with_memory_space_constraint(value, pltpu.VMEM)


def pack(sizes, counts, stored):
    pairs = sizes.pairs
    return pl.pallas_call(
        functools.partial(pack_kernel, sizes),
        out_shape=[in_vmem(sizes.kept, stored)] * (pairs - 1)
        + [
            in_vmem(sizes.passed, stored),
            jax.ShapeDtypeStruct((sizes.adapters + 1,), I32),
            jax.ShapeDtypeStruct((2 * pairs + 3,), I32),
        ],
        in_specs=[IN_SMEM, ANYWHERE],
        out_specs=[IN_VMEM] * pairs + [IN_SMEM, IN_SMEM],
        scratch_shapes=[pltpu.SMEM((pairs,), I32), pltpu.SemaphoreType.DMA((pairs,))],
        compiler_params=PARAMS,
        cost_estimate=SMALL,
        name="pack",
    )(counts, stored)


def pack_again_kernel(sizes, n_after, windows, stored, *refs):
    refs = refs[n_after:]
    pairs = sizes.pairs
    sent, (passed0, kept0, sems) = refs[: pairs - 1], refs[pairs - 1 :]
    copies = [
        pltpu.make_async_copy(stored.at[pl.ds(windows[m], sizes.kept)], target, sems.at[m])
        for m, target in enumerate((kept0,) + tuple(sent))
    ]
    copies.append(
        pltpu.make_async_copy(
            stored.at[pl.ds(windows[pairs], sizes.passed)], passed0, sems.at[pairs]
        )
    )
    for copy in copies:
        copy.start()
    for copy in copies:
        copy.wait()


def pack_again(sizes, windows, stored, after):
    pairs = sizes.pairs
    return pl.pallas_call(
        functools.partial(pack_again_kernel, sizes, len(after)),
        out_shape=[in_vmem(sizes.kept, stored)] * (pairs - 1)
        + [in_vmem(sizes.passed, stored), in_vmem(sizes.kept, stored)],
        in_specs=[IN_SMEM, ANYWHERE] + [ANYWHERE] * len(after),
        out_specs=[IN_VMEM] * (pairs + 1),
        scratch_shapes=[pltpu.SemaphoreType.DMA((pairs + 1,))],
        compiler_params=PARAMS,
        cost_estimate=SMALL,
        name="pack_again",
    )(windows, stored, *after)


def cut_kernel(index, size, n_after, windows, block, *refs):
    out, sem = refs[n_after:]
    copy = pltpu.make_async_copy(block.at[pl.ds(windows[index], size)], out, sem)
    copy.start()
    copy.wait()


def cut(windows, index, block, size, after=()):
    return pl.pallas_call(
        functools.partial(cut_kernel, index, size, len(after)),
        out_shape=in_vmem(size, block),
        in_specs=[IN_SMEM, ANYWHERE] + [ANYWHERE] * len(after),
        out_specs=IN_VMEM,
        scratch_shapes=[pltpu.SemaphoreType.DMA],
        compiler_params=PARAMS,
        cost_estimate=SMALL,
        name="cut",
    )(windows, block, *after)


def gate_kernel(*refs):
    pass


def gate(values, after):
    n = len(values)
    return pl.pallas_call(
        gate_kernel,
        out_shape=[pltpu.VMEM(v.shape, v.dtype) for v in values],
        in_specs=[IN_VMEM] * n + [ANYWHERE] * len(after),
        out_specs=[IN_VMEM] * n,
        input_output_aliases={i: i for i in range(n)},
        compiler_params=PARAMS,
        cost_estimate=SMALL,
        name="gate",
    )(*[held_in_vmem(v) for v in values], *after)


def ranges_kernel(sizes, bounds, windows, ranges, rounds, lows, highs):
    me = lax.axis_index("rollout")
    low_mine = windows[2 * sizes.pairs + 1]
    low = windows[2 * sizes.pairs + 2]
    first_row = me * sizes.rows

    def fill(base, source, start, size):
        for k in range(size):
            adapter = source + sizes.owners * (start + k)
            ranges[2 * (base + k)] = bounds[adapter] - first_row
            ranges[2 * (base + k) + 1] = bounds[adapter + 1] - first_row

    for m in range(sizes.pairs):
        source = me ^ (2 * m)
        fill(sizes.kept_base(m), source, pair_start(source, low_mine, sizes), sizes.kept)
        source = me ^ 1 ^ (2 * m)
        fill(sizes.passed_base(m), source, forward_start(source, low, low_mine, sizes), sizes.passed)

    for d in range(sizes.owners):
        lows[d] = jnp.int32(0)
        highs[d] = jnp.int32(0)

    def count(a, carry):
        end = bounds[a + 1]
        return tuple(
            c + (end <= d * sizes.rows + last).astype(I32)
            for (d, last), c in zip(places, carry)
        )

    places = [(d, last) for last in (0, sizes.rows - 1) for d in range(sizes.owners)]
    found = lax.fori_loop(0, sizes.adapters, count, (jnp.int32(0),) * len(places))
    for d in range(sizes.owners):
        lows[d] = found[d]
        highs[d] = found[sizes.owners + d]

    def most(d, so_far):
        low_d, high_d, low_p = lows[d], highs[d], lows[lax.div(d, jnp.int32(2)) * 2]

        def each(owner, so_far):
            same = ((owner ^ d) & 1) == 0
            covered = jnp.where(
                same,
                pair_start(owner, low_p, sizes) + sizes.kept,
                forward_start(owner, low_d, low_p, sizes) + sizes.passed,
            )
            return jnp.maximum(so_far, end_slot(owner, high_d, sizes.owners) - covered)

        return lax.fori_loop(0, sizes.owners, each, so_far)

    rounds[0] = lax.fori_loop(0, sizes.owners, most, jnp.int32(0))


def ranges_of(sizes, bounds, windows):
    return pl.pallas_call(
        functools.partial(ranges_kernel, sizes),
        out_shape=[
            jax.ShapeDtypeStruct((2 * sizes.slots,), I32),
            jax.ShapeDtypeStruct((1,), I32),
        ],
        in_specs=[IN_SMEM, IN_SMEM],
        out_specs=[IN_SMEM, IN_SMEM],
        scratch_shapes=[pltpu.SMEM((sizes.owners,), I32), pltpu.SMEM((sizes.owners,), I32)],
        compiler_params=PARAMS,
        cost_estimate=SMALL,
        name="ranges",
    )(bounds, windows)


def row_of_lane(rows, steps):
    lane = lax.broadcasted_iota(I32, (1, steps * rows), 1)
    row = lane
    for s in range(1, steps):
        row = jnp.where(lane >= s * rows, lane - s * rows, row)
    return row


def scores_kernel(bases, rank, rows, fold, n_before, n_after, ranges, hidden, *refs):
    blocks, refs = refs[: len(bases)], refs[len(bases) :]
    before, refs = refs[:n_before], refs[n_before + n_after :]
    width = hidden.shape[1]
    tile = min(1024, width)
    total = None
    for k in range(0, width, tile):
        part = lax.dot_general(
            jnp.concatenate([b[:, k : k + tile] for b in blocks], axis=0),
            hidden[:, k : k + tile],
            (((1,), (1,)), ((), ())),
            preferred_element_type=F32,
        )
        total = part if total is None else total + part
    row = row_of_lane(rows, hidden.shape[0] // rows)
    acc = before[0][...] if n_before else jnp.zeros((rank, hidden.shape[0]), F32)
    place = 0
    for base, block in zip(bases, blocks):
        for k in range(block.shape[0] // rank):
            here = (row >= ranges[2 * (base + k)]) & (row < ranges[2 * (base + k) + 1])
            acc = acc + jnp.where(here, total[place : place + rank, :], 0.0)
            place += rank
    if fold:
        refs[1][...] = acc.astype(BF16)
    refs[0][...] = acc


def scores(ranges, hidden, blocks, bases, rows, before=(), after=(), fold=False):
    total_rows, width = hidden.shape
    rank = blocks[0].shape[1]
    flat = [held_in_vmem(b.reshape(-1, width)) for b in blocks]
    out_shape = [pltpu.VMEM((rank, total_rows), F32)]
    if fold:
        out_shape.append(pltpu.VMEM((rank, total_rows), BF16))
    return pl.pallas_call(
        functools.partial(scores_kernel, bases, rank, rows, fold, len(before), len(after)),
        out_shape=out_shape,
        in_specs=[IN_SMEM, IN_VMEM]
        + [IN_VMEM] * (len(flat) + len(before))
        + [ANYWHERE] * len(after),
        out_specs=[IN_VMEM] * len(out_shape),
        compiler_params=PARAMS,
        cost_estimate=SMALL,
        name="scores",
    )(ranges, hidden, *flat, *[held_in_vmem(b) for b in before], *after)


def base_kernel(n_after, which, hidden, weight, *refs):
    refs[n_after][...] = jnp.dot(
        hidden[...], weight[...], preferred_element_type=F32
    ).astype(BF16)


def base_product(which, hidden, weight, columns, after):
    total_rows, width = hidden.shape
    tile = min(256, columns)
    tiles = columns // tile
    return pl.pallas_call(
        functools.partial(base_kernel, len(after)),
        grid_spec=pltpu.PrefetchScalarGridSpec(
            num_scalar_prefetch=1,
            grid=(tiles,),
            in_specs=[
                IN_VMEM,
                pl.BlockSpec((width, tile), lambda j, which: (0, which[0] * tiles + j)),
            ]
            + [ANYWHERE] * len(after),
            out_specs=pl.BlockSpec((total_rows, tile), lambda j, which: (0, j)),
        ),
        out_shape=jax.ShapeDtypeStruct((total_rows, columns), BF16),
        compiler_params=PARAMS,
        cost_estimate=SMALL,
        name="base_product",
    )(which, hidden, pltpu.with_memory_space_constraint(weight, pltpu.HBM), *after)


def spread_kernel(slots, rank, rows, ranges, own, got, out):
    row = row_of_lane(rows, own.shape[1] // rows)
    proj = own[...] + got[...].astype(F32)
    for k in range(slots):
        here = (row >= ranges[2 * k]) & (row < ranges[2 * k + 1])
        out[k * rank : (k + 1) * rank, :] = jnp.where(here, proj, 0.0).astype(BF16)


def spread(slots, rank, rows, ranges, own, got):
    return pl.pallas_call(
        functools.partial(spread_kernel, slots, rank, rows),
        out_shape=pltpu.VMEM((slots * rank, own.shape[1]), BF16),
        in_specs=[IN_SMEM, IN_VMEM, IN_VMEM],
        out_specs=IN_VMEM,
        compiler_params=PARAMS,
        cost_estimate=SMALL,
        name="spread",
    )(ranges, held_in_vmem(own), held_in_vmem(got))


def final_kernel(n_added, left, *refs):
    added, blocks, (out, held, sems) = refs[:n_added], refs[n_added:-3], refs[-3:]
    tile = held.shape[2]
    copies = []
    for j in range(held.shape[0]):
        here = slice(j * tile, (j + 1) * tile)
        total = lax.dot_general(
            left[...],
            jnp.concatenate([b[:, here] for b in blocks], axis=0),
            (((0,), (0,)), ((), ())),
            preferred_element_type=F32,
        )
        for term in added:
            total = total + term[:, here].astype(F32)
        held[j] = total.astype(BF16)
        copy = pltpu.make_async_copy(held.at[j], out.at[:, pl.ds(j * tile, tile)], sems.at[j])
        copy.start()
        copies.append(copy)
    for copy in copies:
        copy.wait()


def final(left, added, blocks):
    total_rows = left.shape[1]
    columns = blocks[0].shape[2]
    flat = [held_in_vmem(b.reshape(-1, columns)) for b in blocks]
    tile = min(256, columns)
    tiles = columns // tile
    return pl.pallas_call(
        functools.partial(final_kernel, len(added)),
        out_shape=jax.ShapeDtypeStruct((total_rows, columns), BF16),
        in_specs=[IN_VMEM] * (1 + len(added) + len(flat)),
        out_specs=ANYWHERE,
        scratch_shapes=[
            pltpu.VMEM((tiles, total_rows, tile), BF16),
            pltpu.SemaphoreType.DMA((tiles,)),
        ],
        compiler_params=PARAMS,
        cost_estimate=SMALL,
        name="final",
    )(held_in_vmem(left), *[held_in_vmem(a) for a in added], *flat)


def send(value, hop, owners):
    return lax.ppermute(value, "rollout", [(i, i ^ hop) for i in range(owners)])


class Extra:

    def __init__(self, sizes, counts):
        rows, owners = sizes.rows, sizes.owners
        self.sizes = sizes
        self.me = lax.axis_index("rollout")
        order = jnp.arange(sizes.adapters, dtype=I32)
        bounds = jnp.sum(jnp.where(order[:, None] <= order[None, :], counts[:, None], 0), axis=0)

        def at_most(positions):
            return jnp.sum((bounds <= positions[:, None]).astype(I32), axis=-1)

        self.row_adapter = at_most(self.me * rows + jnp.arange(rows, dtype=I32))
        device = jnp.arange(owners, dtype=I32)
        low = at_most(device * rows)
        owner = device[:, None]
        low_pair = low[device // 2 * 2][None, :]
        self.covered = jnp.where(
            (owner % 2) == (device[None, :] % 2),
            pair_start(owner, low_pair, sizes) + sizes.kept,
            forward_start(owner, low[None, :], low_pair, sizes) + sizes.passed,
        )

    def blocks(self, stored, turn):
        sizes, me = self.sizes, self.me
        blocks, adapters = [], []
        for hop in range(sizes.owners):
            wanted = jnp.minimum(self.covered[me, me ^ hop] + turn, sizes.held - 1)
            block = lax.dynamic_slice_in_dim(stored, wanted, 1, axis=0)
            blocks.append(block if hop == 0 else send(block, hop, sizes.owners))
            source = me ^ hop
            slot = self.covered[source, me] + turn
            adapters.append(jnp.where(slot < sizes.held, source + sizes.owners * slot, -1))
        return jnp.concatenate(blocks), self.row_adapter[:, None] == jnp.stack(adapters)[None, :]

    def more_rank(self, hidden, down, turn, total):
        blocks, mask = self.blocks(down, turn)
        rank = blocks.shape[1]
        every = jnp.einsum("srd,nkd->srnk", hidden, blocks, preferred_element_type=F32)
        more = jnp.sum(every * mask[None, :, :, None].astype(F32), axis=2)
        return total + more.transpose(2, 0, 1).reshape(total.shape)

    def more_delta(self, rank_proj, up, turn, total):
        blocks, mask = self.blocks(up, turn)
        wide = rank_proj[:, :, None, :] * mask[None, :, :, None].astype(BF16)
        wide = wide.reshape(wide.shape[:2] + (-1,))
        more = jnp.einsum(
            "srw,wc->src",
            wide,
            blocks.reshape(-1, blocks.shape[2]),
            preferred_element_type=F32,
        )
        return total + more.reshape(total.shape)


def local(hidden, counts, key_value_weight, down, up):
    steps, rows, width = hidden.shape
    owners = lax.axis_size("rollout")
    sides = lax.axis_size("tensor")
    held, rank = down.shape[:2]
    sizes = Sizes(owners, counts.shape[0], held, rows)
    pairs = sizes.pairs
    side = lax.axis_index("tensor")
    flat = hidden.reshape(steps * rows, width)
    own_columns = key_value_weight.shape[1] // sides

    def swap_sides(value):
        return lax.ppermute(value, "tensor", [(0, 1), (1, 0)])

    hops = [2 * m for m in range(1, pairs)]
    late = [hops[-1]]
    kept_bases = [sizes.kept_base(m) for m in range(pairs)]
    passed_bases = [sizes.passed_base(m) for m in range(pairs)]

    *to_pairs, to_side, bounds, windows = pack(sizes, counts, down)
    near = held_in_vmem(flat)
    from_side = send(to_side, 1, owners)
    from_pairs = [send(b, hop, owners) for b, hop in zip(to_pairs, hops) if hop not in late]
    ranges, extra = ranges_of(sizes, bounds, windows)
    kept0 = cut(windows, 0, down, sizes.kept, after=[ranges])

    if sides == 2:
        side_index = jnp.reshape(side, (1,)).astype(I32)
        theirs = base_product(1 - side_index, near, key_value_weight, own_columns, [kept0])
        to_pairs[-1:] = gate(to_pairs[-1:], [theirs, from_side])
        added = [swap_sides(theirs)]
        mine = base_product(side_index, near, key_value_weight, own_columns, to_pairs[-1:])
        added.append(mine)
    else:
        partial = jnp.dot(flat, key_value_weight, preferred_element_type=F32).astype(BF16)
        added = [lax.psum_scatter(partial, "tensor", scatter_dimension=1, tiled=True)]
        mine = added[0]
    from_pairs.append(send(to_pairs[-1], hops[-1], owners))

    group_count = lax.axis_size("groups")
    rounds = extra
    for turn in range(1, group_count):
        around = [(i, (i + turn) % group_count) for i in range(group_count)]
        rounds = jnp.maximum(rounds, lax.ppermute(extra, "groups", around))
    more = rounds[0] > 0

    kept, passed = [kept0] + from_pairs, [from_side]
    before, order = (), [mine, rounds]
    for m in range(1, pairs):
        if m == pairs - 1:
            *to_pairs_up, to_side_up, kept_up = pack_again(sizes, windows, up, order)
            order = [kept_up]
        part = cut(windows, pairs + 1 + m, kept[m], sizes.passed, order)
        passed.append(send(part, 1, owners))
        if m == pairs - 1:
            to_side_up, *to_pairs_up = gate([to_side_up, *to_pairs_up], [part])
            order = [to_side_up]
        else:
            order = [part]
        blocks, bases = [kept[m], passed[m - 1]], [kept_bases[m], passed_bases[m - 1]]
        if m == 1:
            blocks, bases = [kept0] + blocks, kept_bases[:1] + bases
        before = scores(ranges, near, blocks, bases, rows, before, order)
        order = before
    own, sent = scores(ranges, near, passed[-1:], passed_bases[-1:], rows, before, fold=True)

    def over_sides(own, sent):
        if sides == 2:
            return own, swap_sides(sent)
        return jnp.zeros_like(own), lax.psum(sent, "tensor")

    from_pairs_up = [send(b, hop, owners) for hop, b in zip(hops, to_pairs_up)]
    ups = [kept_up] + from_pairs_up + [send(to_side_up, 1, owners)]
    order = [sent]
    for m in range(1, pairs):
        part = cut(windows, pairs + 1 + m, from_pairs_up[m - 1], sizes.passed, order)
        order = [part]
        ups.append(send(part, 1, owners))
    spread_out = functools.partial(spread, sizes.slots, rank, rows, ranges)

    def with_rest():
        rest = Extra(sizes, counts)
        more_rank = functools.partial(rest.more_rank, hidden, down)
        total = lax.fori_loop(0, rounds[0], more_rank, own)
        total, got = over_sides(total, total.astype(BF16))
        proj = (total + got.astype(F32)).astype(BF16)
        proj = proj.reshape(rank, steps, rows).transpose(1, 2, 0)
        more_delta = functools.partial(rest.more_delta, proj, up)
        delta = lax.fori_loop(0, rounds[0], more_delta, jnp.zeros(added[0].shape, F32))
        return final(spread_out(total, got), added + [delta], ups)

    left = spread_out(*over_sides(own, sent))
    out = lax.cond(more, with_rest, lambda: final(left, added, ups))
    return out.reshape(steps, rows, own_columns).transpose(2, 0, 1)


def solution(mesh):
    placed = (
        P(None, ("groups", "rollout"), "tensor"),
        P("groups"),
        P("tensor", None),
        P(("groups", "rollout"), None, "tensor"),
        P(("groups", "rollout"), None, "tensor"),
    )
    return jax.shard_map(
        local,
        mesh=mesh,
        in_specs=placed,
        out_specs=P("tensor", None, ("groups", "rollout")),
        check_vma=False,
    )
```

```python
import functools

import jax
import jax.numpy as jnp
from jax import lax
from jax.experimental import pallas as pl
from jax.experimental.pallas import tpu as pltpu
from jax.sharding import PartitionSpec as P

PAIR_SLOTS = 3
FORWARD_SLOTS = 2
BF16 = jnp.bfloat16
F32 = jnp.float32
I32 = jnp.int32
SMALL = pl.CostEstimate(flops=1000, bytes_accessed=1000, transcendentals=0)
MIB = 1024 * 1024
PARAMS = pltpu.CompilerParams(vmem_limit_bytes=8 * MIB)
WIDE_PARAMS = pltpu.CompilerParams(vmem_limit_bytes=22 * MIB)
IN_SMEM = pl.BlockSpec(memory_space=pltpu.SMEM)
IN_VMEM = pl.BlockSpec(memory_space=pltpu.VMEM)
ANYWHERE = pl.BlockSpec(memory_space=pl.ANY)


def first_slot(owner, adapter, owners):
    return lax.div(adapter - owner + (owners - 1), jnp.int32(owners))


def end_slot(owner, adapter, owners):
    return lax.div(adapter - owner + owners, jnp.int32(owners))


def pair_start(owner, pair, lows, sizes):
    own = jnp.minimum(first_slot(owner, lows(pair), sizes.owners), sizes.held - sizes.kept)
    base = jnp.minimum(first_slot(owner, lows(pair & -2), sizes.owners), sizes.held - sizes.kept)
    apart = (owner >> 2) != (pair >> 1)
    second = (pair & 1) == 1
    return jnp.where(apart & second, jnp.minimum(own, base + (sizes.kept - 1)), own)


def own_start(owner, low, size, sizes):
    return jnp.minimum(first_slot(owner, low, sizes.owners), sizes.held - size)


def forward_start(owner, low, start, sizes):
    return jnp.minimum(
        first_slot(owner, low, sizes.owners), start + (sizes.kept - sizes.passed)
    )


class Sizes:
    def __init__(self, owners, counts, down, up, rows):
        self.owners, self.adapters, self.rows = owners, counts.shape[0], rows
        self.held, self.rank, self.columns = up.shape
        self.parts = down.shape[2] // self.columns
        self.kept, self.passed = PAIR_SLOTS, FORWARD_SLOTS
        self.direct = self.kept - 1
        self.pairs = owners // 2
        self.slots = self.pairs * (self.kept + self.passed)
        self.split = [m for m in range(2, self.pairs) if m % 2 == 0]
        self.whole = [m for m in range(self.pairs - 1, 0, -1) if m not in self.split]
        self.forward_at = self.pairs + 1
        self.third_at = 2 * self.pairs + 1
        self.scalars = 3 * self.pairs + 2

    def kept_base(self, m):
        return m * self.kept

    def passed_base(self, m):
        return self.pairs * self.kept + m * self.passed

    def is_split(self, m):
        return m in self.split


def bring(sizes, down, up, start, target, sems, copies):
    size, parts = target.shape[:2]
    for c in range(parts):
        if c < sizes.parts:
            piece = down.at[pl.ds(start, size), :, pl.ds(c * sizes.columns, sizes.columns)]
        else:
            piece = up.at[pl.ds(start, size)]
        copies.append(pltpu.make_async_copy(piece, target.at[:, c], sems.at[len(copies)]))
        copies[-1].start()


def pack_kernel(sizes, counts, down, up, *refs):
    pairs = sizes.pairs
    sent = dict(zip(sizes.whole, refs))
    passed0, bounds, windows, low_pair, sems = refs[len(sent) :]
    me = lax.axis_index("rollout")
    mine = me >> 1
    odd_row = (2 * mine + 1) * sizes.rows
    bounds[0] = jnp.int32(0)

    def add(a, carry):
        end = carry[0] + counts[a]
        bounds[a + 1] = end
        lows = [
            low + (end <= 2 * p * sizes.rows).astype(I32) for p, low in enumerate(carry[1 : pairs + 1])
        ]
        return (end, *lows, carry[pairs + 1] + (end <= odd_row).astype(I32))

    found = lax.fori_loop(0, sizes.adapters, add, (jnp.int32(0),) * (pairs + 2), unroll=8)
    for p in range(pairs):
        low_pair[p] = found[1 + p]
    odd = found[pairs + 1]

    def lows(p):
        return low_pair[p]

    copies = []
    is_even = (me & 1) == 0
    low_other = jnp.where(is_even, odd, low_pair[mine])
    low_me = jnp.where(is_even, low_pair[mine], odd)
    for m in sizes.whole + sizes.split:
        start = pair_start(me, mine ^ m, lows, sizes)
        windows[m] = start
        if m in sent:
            bring(sizes, down, up, start, sent[m], sems, copies)
    start = own_start(me, low_other, sizes.passed, sizes)
    windows[pairs] = start
    bring(sizes, down, up, start, passed0, sems, copies)
    windows[0] = own_start(me, low_me, sizes.kept, sizes)
    windows[sizes.forward_at] = jnp.int32(0)
    windows[sizes.third_at] = jnp.int32(0)
    for m in range(1, pairs):
        source = me ^ (2 * m)
        start = pair_start(source, mine, lows, sizes)
        windows[sizes.forward_at + m] = forward_start(source, low_other, start, sizes) - start
        beside = mine ^ 1
        third = pair_start(source, beside, lows, sizes) + jnp.where(
            (beside & 1) == 0, sizes.direct, 0
        )
        windows[sizes.third_at + m] = jnp.clip(third - start, 0, sizes.kept - 1)
    windows[sizes.scalars - 1] = mine & 1
    for copy in copies:
        copy.wait()


def held_in_vmem(value):
    return pltpu.with_memory_space_constraint(value, pltpu.VMEM)


def slots_in_vmem(sizes, slots, parts):
    return pltpu.VMEM((slots, parts, sizes.rank, sizes.columns), BF16)


def pack(sizes, counts, down, up):
    pairs, parts = sizes.pairs, sizes.parts
    return pl.pallas_call(
        functools.partial(pack_kernel, sizes),
        out_shape=[slots_in_vmem(sizes, sizes.kept, parts + 1)] * len(sizes.whole)
        + [
            slots_in_vmem(sizes, sizes.passed, parts + 1),
            jax.ShapeDtypeStruct((sizes.adapters + 1,), I32),
            jax.ShapeDtypeStruct((sizes.scalars,), I32),
        ],
        in_specs=[IN_SMEM, ANYWHERE, ANYWHERE],
        out_specs=[IN_VMEM] * (len(sizes.whole) + 1) + [IN_SMEM, IN_SMEM],
        scratch_shapes=[
            pltpu.SMEM((pairs,), I32),
            pltpu.SemaphoreType.DMA(((pairs + 1) * (parts + 1),)),
        ],
        compiler_params=PARAMS,
        cost_estimate=SMALL,
        name="pack",
    )(counts, down, up)


def pack_more_kernel(sizes, m, n_after, windows, down, up, *refs):
    target, sems = refs[n_after:]
    start = windows[m]
    if sizes.is_split(m):
        start = start + windows[sizes.scalars - 1]
    copies = []
    bring(sizes, down, up, start, target, sems, copies)
    for copy in copies:
        copy.wait()


def pack_more(sizes, m, windows, down, up, after):
    parts = sizes.parts
    shape = (sizes.direct, parts) if sizes.is_split(m) else (sizes.kept, parts + 1)
    return pl.pallas_call(
        functools.partial(pack_more_kernel, sizes, m, len(after)),
        out_shape=slots_in_vmem(sizes, *shape),
        in_specs=[IN_SMEM, ANYWHERE, ANYWHERE] + [ANYWHERE] * len(after),
        out_specs=IN_VMEM,
        scratch_shapes=[pltpu.SemaphoreType.DMA((parts + 1,))],
        compiler_params=PARAMS,
        cost_estimate=SMALL,
        name="pack_more",
    )(windows, down, up, *after)


def collect_kernel(places, n_after, *refs):
    blocks, (out, sems) = refs[: len(places)], refs[len(places) + n_after :]
    copies, at = [], 0
    for block, c in zip(blocks, places):
        size = block.shape[0]
        copies.append(
            pltpu.make_async_copy(
                block.at[:, c], out.at[pl.ds(at, size), 0], sems.at[len(copies)]
            )
        )
        copies[-1].start()
        at += size
    for copy in copies:
        copy.wait()


def collect(sizes, blocks, after):
    places = [sizes.parts] * len(blocks)
    return pl.pallas_call(
        functools.partial(collect_kernel, places, len(after)),
        out_shape=slots_in_vmem(sizes, sum(b.shape[0] for b in blocks), 1),
        in_specs=[ANYWHERE] * (len(blocks) + len(after)),
        out_specs=IN_VMEM,
        scratch_shapes=[pltpu.SemaphoreType.DMA((len(blocks),))],
        compiler_params=PARAMS,
        cost_estimate=SMALL,
        name="collect",
    )(*blocks, *after)


def pack_up_kernel(sizes, m, n_after, windows, up, *refs):
    target, sems = refs[n_after:]
    second = windows[sizes.scalars - 1]
    third = windows[m] + sizes.direct * (1 - second)
    copies = [
        pltpu.make_async_copy(
            up.at[pl.ds(windows[m] + second, sizes.direct)],
            target.at[pl.ds(0, sizes.direct), 0],
            sems.at[0],
        ),
        pltpu.make_async_copy(
            up.at[pl.ds(third, 1)], target.at[pl.ds(sizes.direct, 1), 0], sems.at[1]
        ),
    ]
    for copy in copies:
        copy.start()
    for copy in copies:
        copy.wait()


def pack_up(sizes, m, windows, up, after):
    return pl.pallas_call(
        functools.partial(pack_up_kernel, sizes, m, len(after)),
        out_shape=slots_in_vmem(sizes, sizes.kept, 1),
        in_specs=[IN_SMEM, ANYWHERE] + [ANYWHERE] * len(after),
        out_specs=IN_VMEM,
        scratch_shapes=[pltpu.SemaphoreType.DMA((2,))],
        compiler_params=PARAMS,
        cost_estimate=SMALL,
        name="pack_up",
    )(windows, up, *after)


def cut_kernel(index, n_after, windows, block, *refs):
    out, sem = refs[n_after:]
    size, parts = out.shape[:2]
    piece = block.at[pl.ds(windows[index], size), pl.ds(0, parts)]
    copy = pltpu.make_async_copy(piece, out, sem)
    copy.start()
    copy.wait()


def cut(sizes, windows, index, block, size, parts, after=()):
    return pl.pallas_call(
        functools.partial(cut_kernel, index, len(after)),
        out_shape=slots_in_vmem(sizes, size, parts),
        in_specs=[IN_SMEM, ANYWHERE] + [ANYWHERE] * len(after),
        out_specs=IN_VMEM,
        scratch_shapes=[pltpu.SemaphoreType.DMA],
        compiler_params=PARAMS,
        cost_estimate=SMALL,
        name="cut",
    )(windows, block, *after)


def join_kernel(forward_at, second_at, third_at, n_after, windows, direct, third, *refs):
    out, sem = refs[n_after:]
    later = windows[forward_at] == 1
    second = windows[second_at] == 1
    third = third.at[pl.ds(third_at, 1)]

    def take(first, last):
        one = pltpu.make_async_copy(first, out.at[pl.ds(0, 1)], sem.at[0])
        two = pltpu.make_async_copy(last, out.at[pl.ds(1, 1)], sem.at[1])
        one.start()
        two.start()
        one.wait()
        two.wait()

    end = jnp.logical_and(later, jnp.logical_not(second))
    front = jnp.logical_and(jnp.logical_not(later), second)
    first, last = direct.at[pl.ds(0, 1)], direct.at[pl.ds(1, 1)]

    @pl.when(end)
    def _():
        take(last, third)

    @pl.when(front)
    def _():
        take(third, first)

    @pl.when(jnp.logical_not(jnp.logical_or(end, front)))
    def _():
        take(first, last)


def join(sizes, windows, m, direct, third, third_at, after=()):
    return pl.pallas_call(
        functools.partial(
            join_kernel, sizes.forward_at + m, sizes.scalars - 1, third_at, len(after)
        ),
        out_shape=slots_in_vmem(sizes, sizes.passed, direct.shape[1]),
        in_specs=[IN_SMEM, ANYWHERE, ANYWHERE] + [ANYWHERE] * len(after),
        out_specs=IN_VMEM,
        scratch_shapes=[pltpu.SemaphoreType.DMA((2,))],
        compiler_params=PARAMS,
        cost_estimate=SMALL,
        name="join",
    )(windows, direct, third, *after)


def gate_kernel(*refs):
    pass


def gate(values, after):
    n = len(values)
    return pl.pallas_call(
        gate_kernel,
        out_shape=[pltpu.VMEM(v.shape, v.dtype) for v in values],
        in_specs=[IN_VMEM] * n + [ANYWHERE] * len(after),
        out_specs=[IN_VMEM] * n,
        input_output_aliases={i: i for i in range(n)},
        compiler_params=PARAMS,
        cost_estimate=SMALL,
        name="gate",
    )(*[held_in_vmem(v) for v in values], *after)


def ranges_kernel(sizes, bounds, windows, ranges, needs, lows, highs):
    me = lax.axis_index("rollout")
    mine = me >> 1
    first_row = me * sizes.rows

    places = [(d, last) for last in (0, sizes.rows - 1) for d in range(sizes.owners)]

    def count(a, carry):
        end = bounds[a + 1]
        return tuple(
            c + (end <= d * sizes.rows + last).astype(I32)
            for (d, last), c in zip(places, carry)
        )

    found = lax.fori_loop(0, sizes.adapters, count, (jnp.int32(0),) * len(places))
    for d in range(sizes.owners):
        lows[d] = found[d]
        highs[d] = found[sizes.owners + d]

    def low_pair(p):
        return lows[2 * p]

    def fill(index, source, slot):
        adapter = source + sizes.owners * slot
        ranges[2 * index] = bounds[adapter] - first_row
        ranges[2 * index + 1] = bounds[adapter + 1] - first_row

    for m in range(sizes.pairs):
        source = me ^ (2 * m)
        start = windows[0] if m == 0 else pair_start(source, mine, low_pair, sizes)
        second = mine & 1 if sizes.is_split(m) else 0
        for k in range(sizes.kept):
            slot = start + k
            if sizes.is_split(m):
                slot = start + (k + second if k < sizes.direct else sizes.direct * (1 - second))
            fill(sizes.kept_base(m) + k, source, slot)
        source = me ^ 1 ^ (2 * m)
        if m == 0:
            start = own_start(source, lows[me], sizes.passed, sizes)
        else:
            start = pair_start(source, mine, low_pair, sizes)
            start = forward_start(source, lows[me], start, sizes)
        for k in range(sizes.passed):
            fill(sizes.passed_base(m) + k, source, start + k)

    for hop in range(sizes.owners):

        def most(d, so_far, hop=hop):
            owner = d ^ hop
            past = covered(owner, d, hop, lows[d], low_pair, sizes)
            return jnp.maximum(so_far, end_slot(owner, highs[d], sizes.owners) - past)

        needs[hop] = lax.fori_loop(0, sizes.owners, most, jnp.int32(0))


def covered(owner, device, hop, low, low_pair, sizes):
    if hop == 0:
        return own_start(owner, low, sizes.kept, sizes) + sizes.kept
    if hop == 1:
        return own_start(owner, low, sizes.passed, sizes) + sizes.passed
    start = pair_start(owner, device >> 1, low_pair, sizes)
    if hop % 2 == 0:
        return start + sizes.kept
    return forward_start(owner, low, start, sizes) + sizes.passed


def ranges_of(sizes, bounds, windows):
    return pl.pallas_call(
        functools.partial(ranges_kernel, sizes),
        out_shape=[
            jax.ShapeDtypeStruct((2 * sizes.slots,), I32),
            jax.ShapeDtypeStruct((sizes.owners,), I32),
        ],
        in_specs=[IN_SMEM, IN_SMEM],
        out_specs=[IN_SMEM, IN_SMEM],
        scratch_shapes=[pltpu.SMEM((sizes.owners,), I32), pltpu.SMEM((sizes.owners,), I32)],
        compiler_params=PARAMS,
        cost_estimate=SMALL,
        name="ranges",
    )(bounds, windows)


def row_of_lane(rows, steps):
    lane = lax.broadcasted_iota(I32, (1, steps * rows), 1)
    row = lane
    for s in range(1, steps):
        row = jnp.where(lane >= s * rows, lane - s * rows, row)
    return row


def scores_kernel(bases, rank, rows, fold, n_before, n_after, ranges, hidden, *refs):
    blocks, refs = refs[: len(bases)], refs[len(bases) :]
    before, refs = refs[:n_before], refs[n_before + n_after :]
    out, total = refs[0], refs[-1]
    k = pl.program_id(0)
    part = lax.dot_general(
        jnp.concatenate([b[n, k] for b in blocks for n in range(b.shape[0])], axis=0),
        hidden[...],
        (((1,), (1,)), ((), ())),
        preferred_element_type=F32,
    )

    @pl.when(k == 0)
    def _():
        total[...] = part

    @pl.when(k > 0)
    def _():
        total[...] += part

    @pl.when(k == pl.num_programs(0) - 1)
    def _():
        row = row_of_lane(rows, hidden.shape[0] // rows)
        acc = before[0][...] if n_before else jnp.zeros((rank, hidden.shape[0]), F32)
        place = 0
        for base, block in zip(bases, blocks):
            for n in range(block.shape[0]):
                mask = (row >= ranges[2 * (base + n)]) & (row < ranges[2 * (base + n) + 1])
                acc = acc + jnp.where(mask, total[place : place + rank, :], 0.0)
                place += rank
        out[...] = acc
        if fold:
            refs[1][...] = acc.astype(BF16)


def scores(sizes, ranges, hidden, blocks, bases, before=(), after=(), fold=False):
    total_rows = hidden.shape[0]
    rank, rows = sizes.rank, sizes.rows
    deep = sum(b.shape[0] for b in blocks) * rank
    out_shape = [pltpu.VMEM((rank, total_rows), F32)]
    if fold:
        out_shape.append(pltpu.VMEM((rank, total_rows), BF16))
    return pl.pallas_call(
        functools.partial(scores_kernel, bases, rank, rows, fold, len(before), len(after)),
        grid=(sizes.parts,),
        out_shape=out_shape,
        in_specs=[IN_SMEM, pl.BlockSpec((total_rows, sizes.columns), lambda k: (0, k))]
        + [IN_VMEM] * (len(blocks) + len(before))
        + [ANYWHERE] * len(after),
        out_specs=[IN_VMEM] * len(out_shape),
        scratch_shapes=[pltpu.VMEM((deep, total_rows), F32)],
        compiler_params=WIDE_PARAMS,
        cost_estimate=SMALL,
        name="scores",
    )(ranges, hidden, *map(held_in_vmem, blocks), *map(held_in_vmem, before), *after)


def base_kernel(n_after, which, hidden, weight, *refs):
    refs[n_after][...] = jnp.dot(
        hidden[...], weight[...], preferred_element_type=F32
    ).astype(BF16)


def base_product(which, hidden, weight, columns, after):
    total_rows, width = hidden.shape
    tile = min(256, columns)
    tiles = columns // tile
    return pl.pallas_call(
        functools.partial(base_kernel, len(after)),
        grid_spec=pltpu.PrefetchScalarGridSpec(
            num_scalar_prefetch=1,
            grid=(tiles,),
            in_specs=[
                IN_VMEM,
                pl.BlockSpec((width, tile), lambda j, which: (0, which[0] * tiles + j)),
            ]
            + [ANYWHERE] * len(after),
            out_specs=pl.BlockSpec((total_rows, tile), lambda j, which: (0, j)),
        ),
        out_shape=jax.ShapeDtypeStruct((total_rows, columns), BF16),
        compiler_params=WIDE_PARAMS,
        cost_estimate=SMALL,
        name="base_product",
    )(which, hidden, pltpu.with_memory_space_constraint(weight, pltpu.HBM), *after)


def spread_kernel(slots, rank, rows, ranges, own, got, out):
    row = row_of_lane(rows, own.shape[1] // rows)
    proj = own[...] + got[...].astype(F32)
    for k, slot in enumerate(slots):
        here = (row >= ranges[2 * slot]) & (row < ranges[2 * slot + 1])
        out[k * rank : (k + 1) * rank, :] = jnp.where(here, proj, 0.0).astype(BF16)


def spread(slots, rank, rows, ranges, own, got):
    return pl.pallas_call(
        functools.partial(spread_kernel, slots, rank, rows),
        out_shape=pltpu.VMEM((len(slots) * rank, own.shape[1]), BF16),
        in_specs=[IN_SMEM, IN_VMEM, IN_VMEM],
        out_specs=IN_VMEM,
        compiler_params=PARAMS,
        cost_estimate=SMALL,
        name="spread",
    )(ranges, held_in_vmem(own), held_in_vmem(got))


def final_kernel(n_added, left, *refs):
    added, blocks = refs[:n_added], refs[n_added : -3 - n_added]
    out, held, sems = refs[-3 - n_added], refs[-2 - n_added], refs[-1]
    terms = refs[-1 - n_added : -1]
    tiles, tile, _ = held.shape
    brought = [
        [
            pltpu.make_async_copy(source.at[pl.ds(j * tile, tile)], term.at[j], sems.at[n + 1, j])
            for n, (source, term) in enumerate(zip(added, terms))
        ]
        for j in range(tiles)
    ]
    for copies in brought:
        for copy in copies:
            copy.start()
    right = jnp.concatenate([b[n, 0] for b in blocks for n in range(b.shape[0])], axis=0)
    taken = []
    for j in range(tiles):
        total = lax.dot_general(
            left[:, j * tile : (j + 1) * tile],
            right,
            (((0,), (0,)), ((), ())),
            preferred_element_type=F32,
        )
        for copy, term in zip(brought[j], terms):
            copy.wait()
            total = total + term[j].astype(F32)
        held[j] = total.astype(BF16)
        taken.append(
            pltpu.make_async_copy(held.at[j], out.at[pl.ds(j * tile, tile)], sems.at[0, j])
        )
        taken[-1].start()
    for copy in taken:
        copy.wait()


def final(left, added, blocks):
    total_rows = left.shape[1]
    columns = blocks[0].shape[3]
    tile = 256 if total_rows % 256 == 0 else total_rows
    tiles = total_rows // tile
    return pl.pallas_call(
        functools.partial(final_kernel, len(added)),
        out_shape=jax.ShapeDtypeStruct((total_rows, columns), BF16),
        in_specs=[IN_VMEM] + [ANYWHERE] * len(added) + [IN_VMEM] * len(blocks),
        out_specs=ANYWHERE,
        scratch_shapes=[pltpu.VMEM((tiles, tile, columns), BF16)]
        + [pltpu.VMEM((tiles, tile, columns), a.dtype) for a in added]
        + [pltpu.SemaphoreType.DMA((1 + len(added), tiles))],
        compiler_params=WIDE_PARAMS,
        cost_estimate=SMALL,
        name="final",
    )(held_in_vmem(left), *added, *map(held_in_vmem, blocks))


def send(value, hop, owners):
    return lax.ppermute(value, "rollout", [(i, i ^ hop) for i in range(owners)])


class Extra:

    def __init__(self, sizes, counts):
        rows, owners = sizes.rows, sizes.owners
        self.sizes = sizes
        self.me = lax.axis_index("rollout")
        order = jnp.arange(sizes.adapters, dtype=I32)
        bounds = jnp.sum(jnp.where(order[:, None] <= order[None, :], counts[:, None], 0), axis=0)

        def at_most(positions):
            return jnp.sum((bounds <= positions[:, None]).astype(I32), axis=-1)

        self.row_adapter = at_most(self.me * rows + jnp.arange(rows, dtype=I32))
        self.low = at_most(jnp.arange(owners, dtype=I32) * rows)

    def past(self, owner, device, hop):
        return covered(
            owner, device, hop, self.low[device], lambda p: self.low[2 * p], self.sizes
        )

    def add(self, hop, hidden, down, up, turn, delta):
        sizes, me, source = self.sizes, self.me, self.me ^ hop
        wanted = jnp.minimum(self.past(me, source, hop) + turn, sizes.held - 1)
        slot = self.past(source, me, hop) + turn
        adapter = jnp.where(slot < sizes.held, source + sizes.owners * slot, -1)
        down_block = lax.dynamic_slice_in_dim(down, wanted, 1, axis=0)
        up_block = lax.dynamic_slice_in_dim(up, wanted, 1, axis=0)
        if hop:
            down_block = send(down_block, hop, sizes.owners)
            up_block = send(up_block, hop, sizes.owners)
        part = jnp.einsum("srd,kd->srk", hidden, down_block[0], preferred_element_type=F32)
        here = (self.row_adapter == adapter)[None, :, None]
        part = jnp.where(here, part, 0.0)
        own, got = over_sides(part, part.astype(BF16))
        proj = (own + got.astype(F32)).astype(BF16)
        more = jnp.einsum("srk,kc->src", proj, up_block[0], preferred_element_type=F32)
        return delta + more.reshape(delta.shape)


def swap_sides(value):
    return lax.ppermute(value, "tensor", [(0, 1), (1, 0)])


def over_sides(own, sent):
    if lax.axis_size("tensor") == 2:
        return own, swap_sides(sent)
    return jnp.zeros_like(own), lax.psum(sent, "tensor")


def local(hidden, counts, key_value_weight, down, up):
    steps, rows, width = hidden.shape
    owners = lax.axis_size("rollout")
    sides = lax.axis_size("tensor")
    sizes = Sizes(owners, counts, down, up, rows)
    pairs, rank, parts = sizes.pairs, sizes.rank, sizes.parts
    side = lax.axis_index("tensor")
    flat = hidden.reshape(steps * rows, width)
    own_columns = key_value_weight.shape[1] // sides
    kept_bases = [sizes.kept_base(m) for m in range(pairs)]
    passed_bases = [sizes.passed_base(m) for m in range(pairs)]
    split, far = sizes.split, sizes.whole[:-1]

    *to_pairs, to_side, bounds, windows = pack(sizes, counts, down, up)
    from_pair = {m: send(b, 2 * m, owners) for m, b in zip(sizes.whole, to_pairs)}
    passed, third = {0: send(to_side, 1, owners)}, {}
    ranges, needs = ranges_of(sizes, bounds, windows)

    group_count = lax.axis_size("groups")
    rounds = needs
    for turn in range(1, group_count):
        around = [(i, (i + turn) % group_count) for i in range(group_count)]
        rounds = jnp.maximum(rounds, lax.ppermute(needs, "groups", around))

    side_index = jnp.reshape(side, (1,)).astype(I32)

    def base(index, order):
        return base_product(index, flat, key_value_weight, own_columns, order)

    if sides == 2:
        theirs = base(1 - side_index, [ranges])
        added, order = [swap_sides(theirs)], [theirs]
    else:
        partial = jnp.dot(flat, key_value_weight, preferred_element_type=F32).astype(BF16)
        added = [lax.psum_scatter(partial, "tensor", scatter_dimension=1, tiled=True)]
        order = [ranges]
    def pass_on(m, order):
        part = cut(
            sizes, windows, sizes.forward_at + m, from_pair[m], sizes.passed, parts + 1, order
        )
        passed[m] = send(part, 1, owners)
        return [part]

    use = functools.partial(scores, sizes, ranges, flat)
    own_block = pack_more(sizes, 0, windows, down, up, [*order, rounds])
    order = [own_block]
    if sides == 2:
        added.append(base(side_index, order))
        order = added[-1:]
    order = pass_on(1, order)
    for m in split:
        block = pack_more(sizes, m, windows, down, up, order)
        from_pair[m] = send(block, 2 * m, owners)
        order = [block]
    before = use(
        [own_block, passed[0], from_pair[1]],
        [kept_bases[0], passed_bases[0], kept_bases[1]],
        (),
        order,
    )
    order = list(before)
    late = [(passed[1], passed_bases[1])]
    for m in far:
        part = cut(sizes, windows, sizes.third_at + m, from_pair[m], 1, parts, order)
        third[m - 1] = send(part, 2, owners)
        order = pass_on(m, [part])
        late += [(from_pair[m], kept_bases[m]), (passed[m], passed_bases[m])]

    last_up, passed_up = {}, {}
    for m in split:
        last_up[m] = pack_up(sizes, m, windows, up, order)
        order = [last_up[m]]
    for m in split:
        part = join(sizes, windows, m, from_pair[m], third[m], 0, order)
        passed[m] = send(part, 1, owners)
        order = [part]
        late += [(from_pair[m], kept_bases[m]), (third[m], kept_bases[m] + sizes.direct)]
    gated = gate([last_up[m] for m in split], order)
    for m, block in zip(split, gated):
        last_up[m] = send(block, 2 * m, owners)
    before = use(*map(list, zip(*late)), before, [gated[0]])
    order = before
    for m in split:
        part = join(sizes, windows, m, last_up[m], last_up[m], sizes.direct, order)
        passed_up[m] = send(part, 1, owners)
        order = [part]
    whole = sizes.whole[::-1]
    both = [own_block] + [from_pair[m] for m in whole] + [passed[m] for m in [0] + whole]
    held_up = collect(sizes, both, order)
    own, sent = use(
        [passed[m] for m in split], [passed_bases[m] for m in split], before, [held_up], fold=True
    )

    ups = [held_up] + [last_up[m] for m in split] + [passed_up[m] for m in split]
    slots = []
    for ms, start, size in (
        ([0] + whole, sizes.kept_base, sizes.kept),
        ([0] + whole, sizes.passed_base, sizes.passed),
        (split, sizes.kept_base, sizes.kept),
        (split, sizes.passed_base, sizes.passed),
    ):
        slots += [start(m) + k for m in ms for k in range(size)]
    left = spread(slots, rank, rows, ranges, *over_sides(own, sent))

    def with_rest():
        rest = Extra(sizes, counts)
        delta = jnp.zeros(added[0].shape, F32)
        for hop in range(owners):
            delta = lax.fori_loop(
                0, rounds[hop], functools.partial(rest.add, hop, hidden, down, up), delta
            )
        return final(left, added + [delta], ups)

    more = jnp.max(rounds) > 0
    out = lax.cond(more, with_rest, lambda: final(left, added, ups))
    return out.reshape(steps, rows, own_columns).transpose(2, 0, 1)


def solution(mesh):
    placed = (
        P(None, ("groups", "rollout"), "tensor"),
        P("groups"),
        P("tensor", None),
        P(("groups", "rollout"), None, "tensor"),
        P(("groups", "rollout"), None, "tensor"),
    )
    return jax.shard_map(
        local,
        mesh=mesh,
        in_specs=placed,
        out_specs=P("tensor", None, ("groups", "rollout")),
        check_vma=False,
    )
```

```python
import functools

import jax
import jax.numpy as jnp
from jax import lax
from jax.experimental import pallas as pl
from jax.experimental.pallas import tpu as pltpu
from jax.sharding import PartitionSpec as P

PAIR_SLOTS = 3
FORWARD_SLOTS = 2
BF16 = jnp.bfloat16
F32 = jnp.float32
I32 = jnp.int32
SMALL = pl.CostEstimate(flops=1000, bytes_accessed=1000, transcendentals=0)
MIB = 1024 * 1024
PARAMS = pltpu.CompilerParams(vmem_limit_bytes=8 * MIB)
WIDE_PARAMS = pltpu.CompilerParams(vmem_limit_bytes=22 * MIB)
IN_SMEM = pl.BlockSpec(memory_space=pltpu.SMEM)
IN_VMEM = pl.BlockSpec(memory_space=pltpu.VMEM)
ANYWHERE = pl.BlockSpec(memory_space=pl.ANY)


def first_slot(owner, adapter, owners):
    return lax.div(adapter - owner + (owners - 1), jnp.int32(owners))


def end_slot(owner, adapter, owners):
    return lax.div(adapter - owner + owners, jnp.int32(owners))


def pair_start(owner, pair, lows, sizes):
    own = jnp.minimum(first_slot(owner, lows(pair), sizes.owners), sizes.held - sizes.kept)
    base = jnp.minimum(first_slot(owner, lows(pair & -2), sizes.owners), sizes.held - sizes.kept)
    apart = (owner >> 2) != (pair >> 1)
    second = (pair & 1) == 1
    return jnp.where(apart & second, jnp.minimum(own, base + (sizes.kept - 1)), own)


def own_start(owner, low, size, sizes):
    return jnp.minimum(first_slot(owner, low, sizes.owners), sizes.held - size)


def forward_start(owner, low, start, sizes):
    return jnp.minimum(
        first_slot(owner, low, sizes.owners), start + (sizes.kept - sizes.passed)
    )


class Sizes:
    def __init__(self, owners, counts, down, up, rows):
        self.owners, self.adapters, self.rows = owners, counts.shape[0], rows
        self.held, self.rank, self.columns = up.shape
        self.parts = down.shape[2] // self.columns
        self.kept, self.passed = PAIR_SLOTS, FORWARD_SLOTS
        self.direct = self.kept - 1
        self.pairs = owners // 2
        self.slots = self.pairs * (self.kept + self.passed)
        self.split = [m for m in range(2, self.pairs) if m % 2 == 0]
        self.whole = [m for m in range(self.pairs - 1, 0, -1) if m not in self.split]
        self.forward_at = self.pairs + 1
        self.third_at = 2 * self.pairs + 1
        self.scalars = 3 * self.pairs + 2

    def kept_base(self, m):
        return m * self.kept

    def passed_base(self, m):
        return self.pairs * self.kept + m * self.passed

    def is_split(self, m):
        return m in self.split


def bring(sizes, down, up, start, target, sems, copies):
    size, parts = target.shape[:2]
    for c in range(parts):
        if c < sizes.parts:
            piece = down.at[pl.ds(start, size), :, pl.ds(c * sizes.columns, sizes.columns)]
        else:
            piece = up.at[pl.ds(start, size)]
        copies.append(pltpu.make_async_copy(piece, target.at[:, c], sems.at[len(copies)]))
        copies[-1].start()


def pack_kernel(sizes, counts, down, up, *refs):
    pairs = sizes.pairs
    sent = dict(zip(sizes.whole, refs))
    passed0, bounds, windows, low_pair, sems = refs[len(sent) :]
    me = lax.axis_index("rollout")
    mine = me >> 1
    odd_row = (2 * mine + 1) * sizes.rows
    bounds[0] = jnp.int32(0)

    def add(a, carry):
        end = carry[0] + counts[a]
        bounds[a + 1] = end
        lows = [
            low + (end <= 2 * p * sizes.rows).astype(I32) for p, low in enumerate(carry[1 : pairs + 1])
        ]
        return (end, *lows, carry[pairs + 1] + (end <= odd_row).astype(I32))

    found = lax.fori_loop(0, sizes.adapters, add, (jnp.int32(0),) * (pairs + 2), unroll=8)
    for p in range(pairs):
        low_pair[p] = found[1 + p]
    odd = found[pairs + 1]

    def lows(p):
        return low_pair[p]

    copies = []
    is_even = (me & 1) == 0
    low_other = jnp.where(is_even, odd, low_pair[mine])
    low_me = jnp.where(is_even, low_pair[mine], odd)
    for m in sizes.whole + sizes.split:
        start = pair_start(me, mine ^ m, lows, sizes)
        windows[m] = start
        if m in sent:
            bring(sizes, down, up, start, sent[m], sems, copies)
    start = own_start(me, low_other, sizes.passed, sizes)
    windows[pairs] = start
    bring(sizes, down, up, start, passed0, sems, copies)
    windows[0] = own_start(me, low_me, sizes.kept, sizes)
    windows[sizes.forward_at] = jnp.int32(0)
    windows[sizes.third_at] = jnp.int32(0)
    for m in range(1, pairs):
        source = me ^ (2 * m)
        start = pair_start(source, mine, lows, sizes)
        windows[sizes.forward_at + m] = forward_start(source, low_other, start, sizes) - start
        beside = mine ^ 1
        third = pair_start(source, beside, lows, sizes) + jnp.where(
            (beside & 1) == 0, sizes.direct, 0
        )
        windows[sizes.third_at + m] = jnp.clip(third - start, 0, sizes.kept - 1)
    windows[sizes.scalars - 1] = mine & 1
    for copy in copies:
        copy.wait()


def held_in_vmem(value):
    return pltpu.with_memory_space_constraint(value, pltpu.VMEM)


def slots_in_vmem(sizes, slots, parts):
    return pltpu.VMEM((slots, parts, sizes.rank, sizes.columns), BF16)


def pack(sizes, counts, down, up):
    pairs, parts = sizes.pairs, sizes.parts
    return pl.pallas_call(
        functools.partial(pack_kernel, sizes),
        out_shape=[slots_in_vmem(sizes, sizes.kept, parts + 1)] * len(sizes.whole)
        + [
            slots_in_vmem(sizes, sizes.passed, parts + 1),
            jax.ShapeDtypeStruct((sizes.adapters + 1,), I32),
            jax.ShapeDtypeStruct((sizes.scalars,), I32),
        ],
        in_specs=[IN_SMEM, ANYWHERE, ANYWHERE],
        out_specs=[IN_VMEM] * (len(sizes.whole) + 1) + [IN_SMEM, IN_SMEM],
        scratch_shapes=[
            pltpu.SMEM((pairs,), I32),
            pltpu.SemaphoreType.DMA(((pairs + 1) * (parts + 1),)),
        ],
        compiler_params=PARAMS,
        cost_estimate=SMALL,
        name="pack",
    )(counts, down, up)


def pack_more_kernel(sizes, m, n_after, windows, down, up, *refs):
    target, sems = refs[n_after:]
    start = windows[m]
    if sizes.is_split(m):
        start = start + windows[sizes.scalars - 1]
    copies = []
    bring(sizes, down, up, start, target, sems, copies)
    for copy in copies:
        copy.wait()


def pack_more(sizes, m, windows, down, up, after):
    parts = sizes.parts
    shape = (sizes.direct, parts) if sizes.is_split(m) else (sizes.kept, parts + 1)
    return pl.pallas_call(
        functools.partial(pack_more_kernel, sizes, m, len(after)),
        out_shape=slots_in_vmem(sizes, *shape),
        in_specs=[IN_SMEM, ANYWHERE, ANYWHERE] + [ANYWHERE] * len(after),
        out_specs=IN_VMEM,
        scratch_shapes=[pltpu.SemaphoreType.DMA((parts + 1,))],
        compiler_params=PARAMS,
        cost_estimate=SMALL,
        name="pack_more",
    )(windows, down, up, *after)


def collect_kernel(places, n_after, *refs):
    blocks, (out, sems) = refs[: len(places)], refs[len(places) + n_after :]
    copies, at = [], 0
    for block, c in zip(blocks, places):
        size = block.shape[0]
        copies.append(
            pltpu.make_async_copy(
                block.at[:, c], out.at[pl.ds(at, size), 0], sems.at[len(copies)]
            )
        )
        copies[-1].start()
        at += size
    for copy in copies:
        copy.wait()


def collect(sizes, blocks, after):
    places = [sizes.parts] * len(blocks)
    return pl.pallas_call(
        functools.partial(collect_kernel, places, len(after)),
        out_shape=slots_in_vmem(sizes, sum(b.shape[0] for b in blocks), 1),
        in_specs=[ANYWHERE] * (len(blocks) + len(after)),
        out_specs=IN_VMEM,
        scratch_shapes=[pltpu.SemaphoreType.DMA((len(blocks),))],
        compiler_params=PARAMS,
        cost_estimate=SMALL,
        name="collect",
    )(*blocks, *after)


def pack_up_kernel(sizes, m, n_after, windows, up, *refs):
    target, sems = refs[n_after:]
    second = windows[sizes.scalars - 1]
    third = windows[m] + sizes.direct * (1 - second)
    copies = [
        pltpu.make_async_copy(
            up.at[pl.ds(windows[m] + second, sizes.direct)],
            target.at[pl.ds(0, sizes.direct), 0],
            sems.at[0],
        ),
        pltpu.make_async_copy(
            up.at[pl.ds(third, 1)], target.at[pl.ds(sizes.direct, 1), 0], sems.at[1]
        ),
    ]
    for copy in copies:
        copy.start()
    for copy in copies:
        copy.wait()


def pack_up(sizes, m, windows, up, after):
    return pl.pallas_call(
        functools.partial(pack_up_kernel, sizes, m, len(after)),
        out_shape=slots_in_vmem(sizes, sizes.kept, 1),
        in_specs=[IN_SMEM, ANYWHERE] + [ANYWHERE] * len(after),
        out_specs=IN_VMEM,
        scratch_shapes=[pltpu.SemaphoreType.DMA((2,))],
        compiler_params=PARAMS,
        cost_estimate=SMALL,
        name="pack_up",
    )(windows, up, *after)


def cut_kernel(index, n_after, windows, block, *refs):
    out, sem = refs[n_after:]
    size, parts = out.shape[:2]
    piece = block.at[pl.ds(windows[index], size), pl.ds(0, parts)]
    copy = pltpu.make_async_copy(piece, out, sem)
    copy.start()
    copy.wait()


def cut(sizes, windows, index, block, size, parts, after=()):
    return pl.pallas_call(
        functools.partial(cut_kernel, index, len(after)),
        out_shape=slots_in_vmem(sizes, size, parts),
        in_specs=[IN_SMEM, ANYWHERE] + [ANYWHERE] * len(after),
        out_specs=IN_VMEM,
        scratch_shapes=[pltpu.SemaphoreType.DMA],
        compiler_params=PARAMS,
        cost_estimate=SMALL,
        name="cut",
    )(windows, block, *after)


def join_kernel(forward_at, second_at, third_at, n_after, windows, direct, third, *refs):
    out, sem = refs[n_after:]
    later = windows[forward_at] == 1
    second = windows[second_at] == 1
    third = third.at[pl.ds(third_at, 1)]

    def take(first, last):
        one = pltpu.make_async_copy(first, out.at[pl.ds(0, 1)], sem.at[0])
        two = pltpu.make_async_copy(last, out.at[pl.ds(1, 1)], sem.at[1])
        one.start()
        two.start()
        one.wait()
        two.wait()

    end = jnp.logical_and(later, jnp.logical_not(second))
    front = jnp.logical_and(jnp.logical_not(later), second)
    first, last = direct.at[pl.ds(0, 1)], direct.at[pl.ds(1, 1)]

    @pl.when(end)
    def _():
        take(last, third)

    @pl.when(front)
    def _():
        take(third, first)

    @pl.when(jnp.logical_not(jnp.logical_or(end, front)))
    def _():
        take(first, last)


def join(sizes, windows, m, direct, third, third_at, after=()):
    return pl.pallas_call(
        functools.partial(
            join_kernel, sizes.forward_at + m, sizes.scalars - 1, third_at, len(after)
        ),
        out_shape=slots_in_vmem(sizes, sizes.passed, direct.shape[1]),
        in_specs=[IN_SMEM, ANYWHERE, ANYWHERE] + [ANYWHERE] * len(after),
        out_specs=IN_VMEM,
        scratch_shapes=[pltpu.SemaphoreType.DMA((2,))],
        compiler_params=PARAMS,
        cost_estimate=SMALL,
        name="join",
    )(windows, direct, third, *after)


def gate_kernel(*refs):
    pass


def gate(values, after):
    n = len(values)
    return pl.pallas_call(
        gate_kernel,
        out_shape=[pltpu.VMEM(v.shape, v.dtype) for v in values],
        in_specs=[IN_VMEM] * n + [ANYWHERE] * len(after),
        out_specs=[IN_VMEM] * n,
        input_output_aliases={i: i for i in range(n)},
        compiler_params=PARAMS,
        cost_estimate=SMALL,
        name="gate",
    )(*[held_in_vmem(v) for v in values], *after)


def ranges_kernel(sizes, bounds, windows, ranges, needs, lows, highs):
    me = lax.axis_index("rollout")
    mine = me >> 1
    first_row = me * sizes.rows

    places = [(d, last) for last in (0, sizes.rows - 1) for d in range(sizes.owners)]

    def count(a, carry):
        end = bounds[a + 1]
        return tuple(
            c + (end <= d * sizes.rows + last).astype(I32)
            for (d, last), c in zip(places, carry)
        )

    found = lax.fori_loop(0, sizes.adapters, count, (jnp.int32(0),) * len(places))
    for d in range(sizes.owners):
        lows[d] = found[d]
        highs[d] = found[sizes.owners + d]

    def low_pair(p):
        return lows[2 * p]

    def fill(index, source, slot):
        adapter = source + sizes.owners * slot
        ranges[2 * index] = bounds[adapter] - first_row
        ranges[2 * index + 1] = bounds[adapter + 1] - first_row

    for m in range(sizes.pairs):
        source = me ^ (2 * m)
        start = windows[0] if m == 0 else pair_start(source, mine, low_pair, sizes)
        second = mine & 1 if sizes.is_split(m) else 0
        for k in range(sizes.kept):
            slot = start + k
            if sizes.is_split(m):
                slot = start + (k + second if k < sizes.direct else sizes.direct * (1 - second))
            fill(sizes.kept_base(m) + k, source, slot)
        source = me ^ 1 ^ (2 * m)
        if m == 0:
            start = own_start(source, lows[me], sizes.passed, sizes)
        else:
            start = pair_start(source, mine, low_pair, sizes)
            start = forward_start(source, lows[me], start, sizes)
        for k in range(sizes.passed):
            fill(sizes.passed_base(m) + k, source, start + k)

    for hop in range(sizes.owners):

        def most(d, so_far, hop=hop):
            owner = d ^ hop
            past = covered(owner, d, hop, lows[d], low_pair, sizes)
            return jnp.maximum(so_far, end_slot(owner, highs[d], sizes.owners) - past)

        needs[hop] = lax.fori_loop(0, sizes.owners, most, jnp.int32(0))


def covered(owner, device, hop, low, low_pair, sizes):
    if hop == 0:
        return own_start(owner, low, sizes.kept, sizes) + sizes.kept
    if hop == 1:
        return own_start(owner, low, sizes.passed, sizes) + sizes.passed
    start = pair_start(owner, device >> 1, low_pair, sizes)
    if hop % 2 == 0:
        return start + sizes.kept
    return forward_start(owner, low, start, sizes) + sizes.passed


def ranges_of(sizes, bounds, windows):
    return pl.pallas_call(
        functools.partial(ranges_kernel, sizes),
        out_shape=[
            jax.ShapeDtypeStruct((2 * sizes.slots,), I32),
            jax.ShapeDtypeStruct((sizes.owners,), I32),
        ],
        in_specs=[IN_SMEM, IN_SMEM],
        out_specs=[IN_SMEM, IN_SMEM],
        scratch_shapes=[pltpu.SMEM((sizes.owners,), I32), pltpu.SMEM((sizes.owners,), I32)],
        compiler_params=PARAMS,
        cost_estimate=SMALL,
        name="ranges",
    )(bounds, windows)


def row_of_lane(rows, steps):
    lane = lax.broadcasted_iota(I32, (1, steps * rows), 1)
    row = lane
    for s in range(1, steps):
        row = jnp.where(lane >= s * rows, lane - s * rows, row)
    return row


def scores_kernel(bases, rank, rows, fold, n_before, n_after, staged, ranges, hidden, *refs):
    blocks, refs = refs[: len(bases)], refs[len(bases) :]
    before, refs = refs[:n_before], refs[n_before + n_after :]
    out, total = refs[0], refs[-1]
    k = pl.program_id(0)
    tile = blocks[0].shape[3]
    here = pl.ds(pl.multiple_of(k * tile, tile), tile)
    part = lax.dot_general(
        jnp.concatenate([b[n, k] for b in blocks for n in range(b.shape[0])], axis=0),
        hidden[:, here] if staged else hidden[...],
        (((1,), (1,)), ((), ())),
        preferred_element_type=F32,
    )

    @pl.when(k == 0)
    def _():
        total[...] = part

    @pl.when(k > 0)
    def _():
        total[...] += part

    @pl.when(k == pl.num_programs(0) - 1)
    def _():
        row = row_of_lane(rows, hidden.shape[0] // rows)
        acc = before[0][...] if n_before else jnp.zeros((rank, hidden.shape[0]), F32)
        place = 0
        for base, block in zip(bases, blocks):
            for n in range(block.shape[0]):
                mask = (row >= ranges[2 * (base + n)]) & (row < ranges[2 * (base + n) + 1])
                acc = acc + jnp.where(mask, total[place : place + rank, :], 0.0)
                place += rank
        out[...] = acc
        if fold:
            refs[1][...] = acc.astype(BF16)


def scores(sizes, ranges, hidden, blocks, bases, before=(), after=(), fold=False, staged=False):
    total_rows = hidden.shape[0]
    rank, rows = sizes.rank, sizes.rows
    deep = sum(b.shape[0] for b in blocks) * rank
    out_shape = [pltpu.VMEM((rank, total_rows), F32)]
    if fold:
        out_shape.append(pltpu.VMEM((rank, total_rows), BF16))
    return pl.pallas_call(
        functools.partial(
            scores_kernel, bases, rank, rows, fold, len(before), len(after), staged
        ),
        grid=(sizes.parts,),
        out_shape=out_shape,
        in_specs=[
            IN_SMEM,
            IN_VMEM if staged else pl.BlockSpec((total_rows, sizes.columns), lambda k: (0, k)),
        ]
        + [IN_VMEM] * (len(blocks) + len(before))
        + [ANYWHERE] * len(after),
        out_specs=[IN_VMEM] * len(out_shape),
        scratch_shapes=[pltpu.VMEM((deep, total_rows), F32)],
        compiler_params=WIDE_PARAMS,
        cost_estimate=SMALL,
        name="scores",
    )(ranges, hidden, *map(held_in_vmem, blocks), *map(held_in_vmem, before), *after)


def stage_kernel(n_after, hidden, *refs):
    out, sem = refs[n_after:]
    copy = pltpu.make_async_copy(hidden, out, sem)
    copy.start()
    copy.wait()


def stage(hidden, after):
    return pl.pallas_call(
        functools.partial(stage_kernel, len(after)),
        out_shape=pltpu.VMEM(hidden.shape, hidden.dtype),
        in_specs=[ANYWHERE] * (1 + len(after)),
        out_specs=IN_VMEM,
        scratch_shapes=[pltpu.SemaphoreType.DMA],
        compiler_params=PARAMS,
        cost_estimate=SMALL,
        name="stage",
    )(hidden, *after)


def base_kernel(n_after, which, hidden, weight, *refs):
    refs[n_after][...] = jnp.dot(
        hidden[...], weight[...], preferred_element_type=F32
    ).astype(BF16)


def base_product(which, hidden, weight, columns, after):
    total_rows, width = hidden.shape
    tile = min(256, columns)
    tiles = columns // tile
    return pl.pallas_call(
        functools.partial(base_kernel, len(after)),
        grid_spec=pltpu.PrefetchScalarGridSpec(
            num_scalar_prefetch=1,
            grid=(tiles,),
            in_specs=[
                IN_VMEM,
                pl.BlockSpec((width, tile), lambda j, which: (0, which[0] * tiles + j)),
            ]
            + [ANYWHERE] * len(after),
            out_specs=pl.BlockSpec((total_rows, tile), lambda j, which: (0, j)),
        ),
        out_shape=jax.ShapeDtypeStruct((total_rows, columns), BF16),
        compiler_params=WIDE_PARAMS,
        cost_estimate=SMALL,
        name="base_product",
    )(which, hidden, pltpu.with_memory_space_constraint(weight, pltpu.HBM), *after)


def spread_kernel(slots, rank, rows, ranges, own, got, out):
    row = row_of_lane(rows, own.shape[1] // rows)
    proj = own[...] + got[...].astype(F32)
    for k, slot in enumerate(slots):
        here = (row >= ranges[2 * slot]) & (row < ranges[2 * slot + 1])
        out[k * rank : (k + 1) * rank, :] = jnp.where(here, proj, 0.0).astype(BF16)


def spread(slots, rank, rows, ranges, own, got):
    return pl.pallas_call(
        functools.partial(spread_kernel, slots, rank, rows),
        out_shape=pltpu.VMEM((len(slots) * rank, own.shape[1]), BF16),
        in_specs=[IN_SMEM, IN_VMEM, IN_VMEM],
        out_specs=IN_VMEM,
        compiler_params=PARAMS,
        cost_estimate=SMALL,
        name="spread",
    )(ranges, held_in_vmem(own), held_in_vmem(got))


def final_kernel(n_added, left, *refs):
    added, blocks = refs[:n_added], refs[n_added : -3 - n_added]
    out, held, sems = refs[-3 - n_added], refs[-2 - n_added], refs[-1]
    terms = refs[-1 - n_added : -1]
    tiles, tile, _ = held.shape
    brought = [
        [
            pltpu.make_async_copy(source.at[pl.ds(j * tile, tile)], term.at[j], sems.at[n + 1, j])
            for n, (source, term) in enumerate(zip(added, terms))
        ]
        for j in range(tiles)
    ]
    for copies in brought:
        for copy in copies:
            copy.start()
    right = jnp.concatenate([b[n, 0] for b in blocks for n in range(b.shape[0])], axis=0)
    taken = []
    for j in range(tiles):
        total = lax.dot_general(
            left[:, j * tile : (j + 1) * tile],
            right,
            (((0,), (0,)), ((), ())),
            preferred_element_type=F32,
        )
        for copy, term in zip(brought[j], terms):
            copy.wait()
            total = total + term[j].astype(F32)
        held[j] = total.astype(BF16)
        taken.append(
            pltpu.make_async_copy(held.at[j], out.at[pl.ds(j * tile, tile)], sems.at[0, j])
        )
        taken[-1].start()
    for copy in taken:
        copy.wait()


def final(left, added, blocks):
    total_rows = left.shape[1]
    columns = blocks[0].shape[3]
    tile = 256 if total_rows % 256 == 0 else total_rows
    tiles = total_rows // tile
    return pl.pallas_call(
        functools.partial(final_kernel, len(added)),
        out_shape=jax.ShapeDtypeStruct((total_rows, columns), BF16),
        in_specs=[IN_VMEM] + [ANYWHERE] * len(added) + [IN_VMEM] * len(blocks),
        out_specs=ANYWHERE,
        scratch_shapes=[pltpu.VMEM((tiles, tile, columns), BF16)]
        + [pltpu.VMEM((tiles, tile, columns), a.dtype) for a in added]
        + [pltpu.SemaphoreType.DMA((1 + len(added), tiles))],
        compiler_params=WIDE_PARAMS,
        cost_estimate=SMALL,
        name="final",
    )(held_in_vmem(left), *added, *map(held_in_vmem, blocks))


def send(value, hop, owners):
    return lax.ppermute(value, "rollout", [(i, i ^ hop) for i in range(owners)])


class Extra:

    def __init__(self, sizes, counts):
        rows, owners = sizes.rows, sizes.owners
        self.sizes = sizes
        self.me = lax.axis_index("rollout")
        order = jnp.arange(sizes.adapters, dtype=I32)
        bounds = jnp.sum(jnp.where(order[:, None] <= order[None, :], counts[:, None], 0), axis=0)

        def at_most(positions):
            return jnp.sum((bounds <= positions[:, None]).astype(I32), axis=-1)

        self.row_adapter = at_most(self.me * rows + jnp.arange(rows, dtype=I32))
        self.low = at_most(jnp.arange(owners, dtype=I32) * rows)

    def past(self, owner, device, hop):
        return covered(
            owner, device, hop, self.low[device], lambda p: self.low[2 * p], self.sizes
        )

    def add(self, hop, hidden, down, up, turn, delta):
        sizes, me, source = self.sizes, self.me, self.me ^ hop
        wanted = jnp.minimum(self.past(me, source, hop) + turn, sizes.held - 1)
        slot = self.past(source, me, hop) + turn
        adapter = jnp.where(slot < sizes.held, source + sizes.owners * slot, -1)
        down_block = lax.dynamic_slice_in_dim(down, wanted, 1, axis=0)
        up_block = lax.dynamic_slice_in_dim(up, wanted, 1, axis=0)
        if hop:
            down_block = send(down_block, hop, sizes.owners)
            up_block = send(up_block, hop, sizes.owners)
        part = jnp.einsum("srd,kd->srk", hidden, down_block[0], preferred_element_type=F32)
        here = (self.row_adapter == adapter)[None, :, None]
        part = jnp.where(here, part, 0.0)
        own, got = over_sides(part, part.astype(BF16))
        proj = (own + got.astype(F32)).astype(BF16)
        more = jnp.einsum("srk,kc->src", proj, up_block[0], preferred_element_type=F32)
        return delta + more.reshape(delta.shape)


def swap_sides(value):
    return lax.ppermute(value, "tensor", [(0, 1), (1, 0)])


def over_sides(own, sent):
    if lax.axis_size("tensor") == 2:
        return own, swap_sides(sent)
    return jnp.zeros_like(own), lax.psum(sent, "tensor")


def local(hidden, counts, key_value_weight, down, up):
    steps, rows, width = hidden.shape
    owners = lax.axis_size("rollout")
    sides = lax.axis_size("tensor")
    sizes = Sizes(owners, counts, down, up, rows)
    pairs, rank, parts = sizes.pairs, sizes.rank, sizes.parts
    side = lax.axis_index("tensor")
    flat = hidden.reshape(steps * rows, width)
    own_columns = key_value_weight.shape[1] // sides
    kept_bases = [sizes.kept_base(m) for m in range(pairs)]
    passed_bases = [sizes.passed_base(m) for m in range(pairs)]
    split, far = sizes.split, sizes.whole[:-1]

    *to_pairs, to_side, bounds, windows = pack(sizes, counts, down, up)
    from_pair = {m: send(b, 2 * m, owners) for m, b in zip(sizes.whole, to_pairs)}
    passed, third = {0: send(to_side, 1, owners)}, {}
    ranges, needs = ranges_of(sizes, bounds, windows)

    group_count = lax.axis_size("groups")
    rounds = needs
    for turn in range(1, group_count):
        around = [(i, (i + turn) % group_count) for i in range(group_count)]
        rounds = jnp.maximum(rounds, lax.ppermute(needs, "groups", around))

    side_index = jnp.reshape(side, (1,)).astype(I32)

    def base(index, order):
        return base_product(index, flat, key_value_weight, own_columns, order)

    if sides == 2:
        theirs = base(1 - side_index, [ranges])
        added, order = [swap_sides(theirs)], [theirs]
    else:
        partial = jnp.dot(flat, key_value_weight, preferred_element_type=F32).astype(BF16)
        added = [lax.psum_scatter(partial, "tensor", scatter_dimension=1, tiled=True)]
        order = [ranges]
    def pass_on(m, order):
        part = cut(
            sizes, windows, sizes.forward_at + m, from_pair[m], sizes.passed, parts + 1, order
        )
        passed[m] = send(part, 1, owners)
        return [part]

    use = functools.partial(scores, sizes, ranges, flat)
    own_block = pack_more(sizes, 0, windows, down, up, [*order, rounds, passed[0]])
    order = [own_block]
    if sides == 2:
        added.append(base(side_index, order))
        order = added[-1:]
    order = pass_on(1, order)
    before = use(
        [own_block, passed[0], from_pair[1]],
        [kept_bases[0], passed_bases[0], kept_bases[1]],
        (),
        order,
    )
    order = list(before)
    for m in split:
        block = pack_more(sizes, m, windows, down, up, order)
        from_pair[m] = send(block, 2 * m, owners)
        order = [block]
    order = [*order, passed[1]]
    late = [(passed[1], passed_bases[1])]
    for m in far:
        part = cut(sizes, windows, sizes.third_at + m, from_pair[m], 1, parts, order)
        third[m - 1] = send(part, 2, owners)
        order = pass_on(m, [part])
        late += [(from_pair[m], kept_bases[m]), (passed[m], passed_bases[m])]

    last_up, passed_up = {}, {}
    for m in split:
        last_up[m] = pack_up(sizes, m, windows, up, order)
        order = [last_up[m]]
    for m in split:
        part = join(sizes, windows, m, from_pair[m], third[m], 0, order)
        passed[m] = send(part, 1, owners)
        order = [part]
        late += [(from_pair[m], kept_bases[m]), (third[m], kept_bases[m] + sizes.direct)]
    gated = gate([last_up[m] for m in split], order)
    for m, block in zip(split, gated):
        last_up[m] = send(block, 2 * m, owners)
    before = use(*map(list, zip(*late)), before, [gated[0]])
    whole = sizes.whole[::-1]
    both = [own_block] + [from_pair[m] for m in whole] + [passed[m] for m in [0] + whole]
    held_up = collect(sizes, both, before)
    staged = stage(flat, [held_up])
    order = [staged]
    for m in split:
        part = join(sizes, windows, m, last_up[m], last_up[m], sizes.direct, order)
        passed_up[m] = send(part, 1, owners)
        order = [part]
    own, sent = scores(
        sizes,
        ranges,
        held_in_vmem(staged),
        [passed[m] for m in split],
        [passed_bases[m] for m in split],
        before,
        order,
        fold=True,
        staged=True,
    )
    ups = [held_up] + [last_up[m] for m in split] + [passed_up[m] for m in split]
    slots = []
    for ms, start, size in (
        ([0] + whole, sizes.kept_base, sizes.kept),
        ([0] + whole, sizes.passed_base, sizes.passed),
        (split, sizes.kept_base, sizes.kept),
        (split, sizes.passed_base, sizes.passed),
    ):
        slots += [start(m) + k for m in ms for k in range(size)]
    left = spread(slots, rank, rows, ranges, *over_sides(own, sent))

    def with_rest():
        rest = Extra(sizes, counts)
        delta = jnp.zeros(added[0].shape, F32)
        for hop in range(owners):
            delta = lax.fori_loop(
                0, rounds[hop], functools.partial(rest.add, hop, hidden, down, up), delta
            )
        return final(left, added + [delta], ups)

    more = jnp.max(rounds) > 0
    out = lax.cond(more, with_rest, lambda: final(left, added, ups))
    return out.reshape(steps, rows, own_columns).transpose(2, 0, 1)


def solution(mesh):
    placed = (
        P(None, ("groups", "rollout"), "tensor"),
        P("groups"),
        P("tensor", None),
        P(("groups", "rollout"), None, "tensor"),
        P(("groups", "rollout"), None, "tensor"),
    )
    return jax.shard_map(
        local,
        mesh=mesh,
        in_specs=placed,
        out_specs=P("tensor", None, ("groups", "rollout")),
        check_vma=False,
    )
```
